32 devices in a mesh: layer: 2 (over y), row: 16 (over z, x, core).
Axes of the slice: x: 2, y: 2, z: 4, core: 2. Of those that a mesh axis runs over, the one named last changes fastest.
Arguments:
- query_grads: bfloat16 [4, 512, 4096], P('layer', 'row'), may hold values from -6 to 6
- train_grads: bfloat16 [4, 8192, 4096], P('layer', 'row'), may hold values from -0.023925781 to 0.023925781
- left_inverse: float32 [4, 64, 64], P('layer'), may hold values from -0.75 to 0.75
- right_inverse: float32 [4, 64, 64], P('layer'), may hold values from -0.75 to 0.75
Outputs:
- scores: float32 [512, 8192], P('layer', 'row')
The draws below stay inside these ranges and needn't reach their ends.
All inputs are finite; a program needn't handle non-finite values.
Results may differ from the reference program's by a relative error of at most 0.0029.
Values may be sent and summed in bfloat16 or wider, within the bound.
No kernel may reach another device: no remote copies, remote signals or barrier semaphores. Data moves between devices by JAX's collectives and lax.ppermute only.
A program may use at most 128 MiB of HBM per device.

```python
import jax
import jax.numpy as jnp
from jax import lax

PROJ = 64
FEAT = 4096
LAYERS = 4
TRAIN = 8192
QUERIES = 512


def block_scale(own_key, shape, split, least, largest):
    gain = 1.0
    for position, parts in split:
        draws = jax.random.uniform(jax.random.fold_in(jax.random.fold_in(own_key, 6), position), (parts,), jnp.float32, least / len(split), largest / len(split))
        gain = gain * jnp.repeat(jnp.exp(draws), shape[position] // parts).reshape((-1,) + (1,) * (len(shape) - 1 - position))
    return gain


def bell_draw(own_key, dims, scale, limit, pieces=(), held_as=jnp.bfloat16):
    values = jax.random.normal(own_key, dims, jnp.float32) * scale
    if len(pieces) > 0:
        values = block_scale(own_key, dims, pieces, -0.22, 0.18) * values
    return jnp.clip(values, min=-limit, max=limit).astype(held_as)


def setup_inputs(seed: int = 0) -> dict:
    key_of = jax.random.split(jax.random.key(seed), 5)
    return {
        "query_grads": bell_draw(key_of[0], (LAYERS, QUERIES, FEAT), 1.0, 6.0, ((0, 2), (1, 16))),
        "train_grads": bell_draw(key_of[1], (LAYERS, TRAIN, FEAT), 0.004, 0.023925781, ((0, 2), (1, 16))),
        "left_inverse": bell_draw(key_of[2], (LAYERS, PROJ, PROJ), PROJ ** -0.5, 0.75, ((0, 2),), jnp.float32),
        "right_inverse": bell_draw(key_of[3], (LAYERS, PROJ, PROJ), PROJ ** -0.5, 0.75, ((0, 2),), jnp.float32),
    }


def reference(query_grads, train_grads, left_inverse, right_inverse):
    layers, queries, feat = query_grads.shape
    proj = left_inverse.shape[1]

    def one_layer(total, index):
        query = lax.dynamic_index_in_dim(query_grads, index, 0, keepdims=False)
        train = lax.dynamic_index_in_dim(train_grads, index, 0, keepdims=False)
        left = lax.dynamic_index_in_dim(left_inverse, index, 0, keepdims=False).astype(jnp.float32)
        right = lax.dynamic_index_in_dim(right_inverse, index, 0, keepdims=False).astype(jnp.float32)
        square = query.astype(jnp.float32).reshape(queries, proj, proj)
        rotated = jnp.einsum("ab,qbc,cd->qad", left, square, right, precision=lax.Precision.HIGHEST)
        rotated = rotated.reshape(queries, feat).astype(jnp.bfloat16)
        term = jnp.dot(rotated, train.T, preferred_element_type=jnp.float32)
        return total + term, None

    start = jnp.zeros((queries, train_grads.shape[1]), jnp.float32)
    total, unused = lax.scan(one_layer, start, jnp.arange(layers, dtype=jnp.int32))
    return total
```

```python
import jax
import jax.numpy as jnp
from jax import lax
from jax.experimental import pallas as pl
from jax.experimental.pallas import tpu as pltpu
from jax.sharding import PartitionSpec as P

AXES = ("layer", "row")
VMEM = pl.BlockSpec(memory_space=pltpu.VMEM)


def halves(v):
    top = v.astype(jnp.bfloat16)
    return top, (v - top.astype(jnp.float32)).astype(jnp.bfloat16)


def dot(a, b):
    return jnp.dot(a, b, preferred_element_type=jnp.float32)


def precondition_kernel(query, left, right, out, turned, mixed):
    layers, rows, feat = query.shape
    proj = left.shape[1]
    half = proj // 2
    pairs = feat // 128
    i = lax.broadcasted_iota(jnp.int32, (2 * proj, 2 * proj), 0) // proj
    j = lax.broadcasted_iota(jnp.int32, (2 * proj, 2 * proj), 1) // proj
    diagonal = i == j
    i = lax.broadcasted_iota(jnp.int32, (proj, proj), 0)
    j = lax.broadcasted_iota(jnp.int32, (proj, proj), 1)
    pick = (j == 2 * lax.rem(i, half) + i // half).astype(jnp.bfloat16)
    pick_t = (i == 2 * lax.rem(j, half) + j // half).astype(jnp.bfloat16)
    step = 8
    low = lax.rem(lax.broadcasted_iota(jnp.int32, (pairs, step * 128), 1), 128) < proj
    for l in range(layers):
        wide = jnp.concatenate([right[l], right[l]], axis=1)
        wide = jnp.where(diagonal, jnp.concatenate([wide, wide], axis=0), 0.0)
        rr = jnp.concatenate(halves(wide), axis=0)
        lh, ll = (dot(dot(pick, m).astype(jnp.bfloat16), pick_t).astype(jnp.bfloat16) for m in halves(left[l]))
        lll = jnp.concatenate([lh, ll, lh], axis=1)
        x = jnp.concatenate([query[l, :, k * 128:(k + 1) * 128] for k in range(pairs)], axis=0)
        turned[l] = dot(jnp.concatenate([x, x], axis=1), rr)
        for q0 in range(0, rows, step):
            u = jnp.concatenate([turned[l, pl.ds(q, pairs, stride=rows), :] for q in range(q0, q0 + step)], axis=1)
            v = jnp.concatenate(
                [pltpu.roll(turned[l, pl.ds(q, pairs, stride=rows), :], proj, 1) for q in range(q0, q0 + step)], axis=1
            )
            wh, wl = halves(jnp.concatenate([jnp.where(low, u, v), jnp.where(low, v, u)], axis=0))
            z = dot(lll, jnp.concatenate([wh, wh, wl], axis=0))
            z = jnp.where(low, z[:half], z[half:])
            for n in range(step):
                mixed[l, pl.ds(q0 + n, pairs, stride=rows), :] = z[:, n * 128:(n + 1) * 128]
        for m in range(pairs):
            out[l, :, m * 128:(m + 1) * 128] = mixed[l, m * rows:(m + 1) * rows].astype(jnp.bfloat16)


def precondition(query, left, right):
    layers, rows, feat = query.shape
    scratch = pltpu.VMEM((layers, rows * feat // 128, 128), jnp.float32)
    return pl.pallas_call(
        precondition_kernel,
        out_shape=jax.ShapeDtypeStruct(query.shape, jnp.bfloat16),
        in_specs=[VMEM] * 3,
        out_specs=VMEM,
        scratch_shapes=[scratch, scratch],
        compiler_params=pltpu.CompilerParams(vmem_limit_bytes=16 << 20),
        cost_estimate=pl.CostEstimate(flops=2 << 30, bytes_accessed=4 << 20, transcendentals=0),
        name="precondition",
    )(query, left, right)


def transpose_kernel(train, pass_in, out, pass_out, buffer, sems):
    del pass_in, pass_out
    layers, rows, feat = train.shape
    wide = buffer.shape[2]
    steps = [(l, k) for l in range(layers) for k in range(0, feat, wide)]
    deep = buffer.shape[0]

    def copy(n):
        l, k = steps[n]
        return pltpu.make_async_copy(train.at[l, :, pl.ds(k, wide)], buffer.at[n % deep], sems.at[n % deep])

    for n in range(deep - 1):
        copy(n).start()
    for n, (l, k) in enumerate(steps):
        if n + deep - 1 < len(steps):
            copy(n + deep - 1).start()
        copy(n).wait()
        out[l, k:k + wide, :] = buffer[n % deep].T


def transpose(train, passed):
    layers, rows, feat = train.shape
    wide, deep = 512, 4
    hbm = pl.BlockSpec(memory_space=pl.ANY)
    return pl.pallas_call(
        transpose_kernel,
        out_shape=(jax.ShapeDtypeStruct((layers, feat, rows), train.dtype), jax.ShapeDtypeStruct(passed.shape, passed.dtype)),
        in_specs=[hbm, hbm],
        out_specs=(VMEM, hbm),
        scratch_shapes=[pltpu.VMEM((deep, rows, wide), train.dtype), pltpu.SemaphoreType.DMA((deep,))],
        input_output_aliases={1: 1},
        compiler_params=pltpu.CompilerParams(vmem_limit_bytes=24 << 20),
        cost_estimate=pl.CostEstimate(flops=4 << 30, bytes_accessed=16 << 20, transcendentals=0),
        name="transpose",
    )(train, passed)


def score(turned, queries):
    total = None
    for l in range(turned.shape[0]):
        rows = jnp.concatenate([q[l] for q in queries], axis=0)
        term = dot(rows, turned[l])
        total = term if total is None else total + term
    return total


def chip_at(offset):
    row = lax.axis_index("row")
    chip, core = row // 2, lax.rem(row, 2)
    up, column = chip // 2, lax.rem(chip, 2)
    place = jnp.where(column == 0, up, 7 - up) - offset * (1 - 2 * core)
    place = lax.rem(place + 8, 8)
    return jnp.where(place < 4, 2 * place, 2 * (7 - place) + 1)


def foreign(offset):
    return chip_at(offset) // 4 != lax.axis_index("layer")


def put(out, at, offset, block):
    rows = block.shape[0] // 2
    core = lax.rem(lax.axis_index("row"), 2)
    if offset < 0:
        core = 1 - core
    start = (at - 4 * lax.axis_index("layer")) * 2 * rows
    out[pl.ds(pl.multiple_of(start + core * rows, rows), rows), :] = block[:rows]
    out[pl.ds(pl.multiple_of(start + (1 - core) * rows, rows), rows), :] = block[rows:]


def split(offset, ahead, behind, sent, kept):
    @pl.when(foreign(offset))
    def _():
        sent[...] = ahead[...]
        kept[...] = behind[...]

    @pl.when(jnp.logical_not(foreign(offset)))
    def _():
        sent[...] = behind[...]
        kept[...] = ahead[...]


def plain_kernel(turned, *refs):
    refs[-1][...] = score(turned, refs[:-1])


def second_kernel(turned, *refs):
    *queries, sent, kept, total = refs
    half = sent.shape[0]
    total[...] = score(turned, queries)
    split(2, total.at[:half], total.at[half:], sent, kept)


def third_kernel(turned, first, *refs):
    *queries, sent, kept, total = refs
    half = total.shape[0] // 2
    total[...] = score(turned, queries)
    split(1, first.at[:half], total.at[half:], sent.at[:half], kept.at[:half])
    split(3, total.at[:half], first.at[half:], sent.at[half:], kept.at[half:])


def fourth_kernel(turned, own, *refs):
    *queries, sent, kept, total = refs
    total[...] = score(turned, queries)
    split(4, total, own, sent, kept)


def block_call(kernel, name, rows, total, turned, operands):
    columns = turned.shape[2]
    block = jax.ShapeDtypeStruct((rows, columns), jnp.float32)
    return pl.pallas_call(
        kernel,
        out_shape=(block, block) if total else block,
        in_specs=[VMEM] * (1 + len(operands)),
        out_specs=(VMEM, VMEM) if total else VMEM,
        scratch_shapes=[pltpu.VMEM((total, columns), jnp.float32)] if total else [],
        compiler_params=pltpu.CompilerParams(vmem_limit_bytes=24 << 20),
        cost_estimate=pl.CostEstimate(flops=2 << 30, bytes_accessed=9 << 20, transcendentals=0),
        name=name,
    )(turned, *operands)


def gather_kernel(kept2, got2, kept13, got13, out):
    half = kept2.shape[0]

    def place(offset, kept, got):
        block = kept[...] + got[...]

        @pl.when(foreign(offset))
        def _():
            put(out, chip_at(offset - 4), offset - 4, block)

        @pl.when(jnp.logical_not(foreign(offset)))
        def _():
            put(out, chip_at(offset), offset, block)

    place(2, kept2, got2)
    place(1, kept13.at[:half], got13.at[:half])
    place(3, kept13.at[half:], got13.at[half:])


def last_kernel(kept, got, table, out, block, sems):
    del table
    rows = kept.shape[0] // 2
    block[...] = kept[...] + got[...]
    at = jnp.where(foreign(4), chip_at(0), chip_at(4)) - 4 * lax.axis_index("layer")
    core = lax.rem(lax.axis_index("row"), 2)
    copies = []
    for n, c in enumerate((core, 1 - core)):
        start = pl.multiple_of((2 * at + c) * rows, rows)
        copies.append(pltpu.make_async_copy(block.at[n * rows:(n + 1) * rows], out.at[pl.ds(start, rows)], sems.at[n]))
    for copy in copies:
        copy.start()
    for copy in copies:
        copy.wait()


def finish(parts, rows, columns):
    (kept2, got2), (kept13, got13), (kept4, got4) = parts
    hbm = pl.BlockSpec(memory_space=pl.ANY)
    table = jax.ShapeDtypeStruct((rows, columns), jnp.float32)
    params = pltpu.CompilerParams(vmem_limit_bytes=8 << 20)
    most = pl.pallas_call(
        gather_kernel, out_shape=table, in_specs=[VMEM] * 4, out_specs=VMEM, compiler_params=params, name="gather_rows"
    )(kept2, got2, kept13, got13)
    return pl.pallas_call(
        last_kernel,
        out_shape=table,
        in_specs=[VMEM, VMEM, hbm],
        out_specs=hbm,
        scratch_shapes=[pltpu.VMEM(kept4.shape, jnp.float32), pltpu.SemaphoreType.DMA((2,))],
        input_output_aliases={2: 0},
        compiler_params=params,
        name="last_rows",
    )(kept4, got4, most)


def ring_order(chips):
    half = chips // 2
    return [2 * i for i in range(half)] + [2 * i + 1 for i in reversed(range(half))]


def ring_device(query_grads, train_grads, left_inverse, right_inverse):
    chips, groups, cores = 8, 2, 2
    order = ring_order(chips)
    flat = lambda layer, chip, core: (layer * chips + chip) * cores + core
    every = [(y, h, c) for y in range(groups) for h in range(chips) for c in range(cores)]
    step = lambda h, c: order[(order.index(h) + (1 - 2 * c)) % chips]
    swap = [(flat(y, h, c), flat(y, h, 1 - c)) for y, h, c in every]
    across = [(flat(y, h, c), flat(1 - y, h, c)) for y, h, c in every]
    around = [(flat(y, h, c), flat(y, step(h, c), c)) for y, h, c in every]
    send = lambda v, pairs: lax.ppermute(v, AXES, pairs)

    mine = precondition(query_grads, left_inverse, right_inverse)
    theirs = send(mine, swap)
    held = [mine, theirs]
    turned, theirs_after = transpose(train_grads, theirs)
    held = [mine, theirs_after]
    rows = 2 * mine.shape[1]
    zeroth = block_call(plain_kernel, "scores_0", rows, 0, turned, held)
    pairs = []
    for k in range(1, 4):
        held = [send(h, around) for h in held]
        queries = held + [send(h, swap) for h in held]
        if k == 1:
            first = block_call(plain_kernel, "scores_1", 2 * rows, 0, turned, queries)
            continue
        if k == 2:
            sent, kept = block_call(second_kernel, "scores_2", rows, 2 * rows, turned, queries)
        else:
            sent, kept = block_call(third_kernel, "scores_3", 2 * rows, 2 * rows, turned, [first] + queries)
        pairs.append((kept, send(sent, across)))
    end = send(held[0], around)
    sent, kept = block_call(fourth_kernel, "scores_4", rows, rows, turned, [zeroth, end, send(end, swap)])
    pairs.append((kept, send(sent, across)))
    return finish(pairs, chips // groups * rows, turned.shape[2])


def on_device(query_grads, train_grads, left_inverse, right_inverse):
    layers, rows, feat = query_grads.shape
    proj = left_inverse.shape[1]
    square = query_grads.astype(jnp.float32).reshape(layers, rows, proj, proj)
    rotated = jnp.einsum(
        "lab,lqbc,lcd->lqad", left_inverse, square, right_inverse, precision=lax.Precision.HIGHEST
    )
    rotated = rotated.reshape(layers, rows, feat).astype(jnp.bfloat16)
    partial_value = jnp.einsum(
        "lqf,ltf->qt",
        lax.all_gather(rotated, "row", axis=1, tiled=True),
        train_grads,
        preferred_element_type=jnp.float32,
    )
    return lax.psum_scatter(partial_value, "layer", scatter_dimension=0, tiled=True)


def solution(mesh):
    placed = (
        P("layer", "row", None),
        P("layer", "row", None),
        P("layer", None, None),
        P("layer", None, None),
    )
    ring = mesh.shape["layer"] == 2 and mesh.shape["row"] == 16
    return jax.shard_map(
        ring_device if ring else on_device, mesh=mesh, in_specs=placed, out_specs=P("layer", "row"), check_vma=False
    )
```

```python
import functools

import jax
import jax.numpy as jnp
from jax import lax
from jax.experimental import pallas as pl
from jax.experimental.pallas import tpu as pltpu
from jax.sharding import PartitionSpec as P

AXES = ("layer", "row")
VMEM = pl.BlockSpec(memory_space=pltpu.VMEM)
HBM = pl.BlockSpec(memory_space=pl.ANY)


def halves(v):
    top = v.astype(jnp.bfloat16)
    return top, (v - top.astype(jnp.float32)).astype(jnp.bfloat16)


def dot(a, b):
    return jnp.dot(a, b, preferred_element_type=jnp.float32)


def precondition_kernel(query_hbm, left_hbm, right_hbm, out, query, left, right, turned, mixed, sems):
    copies = [
        pltpu.make_async_copy(src, dst, sems.at[n])
        for n, (src, dst) in enumerate(((left_hbm, left), (right_hbm, right), (query_hbm, query)))
    ]
    for copy in copies:
        copy.start()
    copies[0].wait()
    copies[1].wait()
    layers, rows, feat = query.shape
    proj = left.shape[1]
    half = proj // 2
    pairs = feat // 128
    i = lax.broadcasted_iota(jnp.int32, (2 * proj, 2 * proj), 0) // proj
    j = lax.broadcasted_iota(jnp.int32, (2 * proj, 2 * proj), 1) // proj
    diagonal = i == j
    i = lax.broadcasted_iota(jnp.int32, (proj, proj), 0)
    j = lax.broadcasted_iota(jnp.int32, (proj, proj), 1)
    pick = (j == 2 * lax.rem(i, half) + i // half).astype(jnp.bfloat16)
    pick_t = (i == 2 * lax.rem(j, half) + j // half).astype(jnp.bfloat16)
    copies[2].wait()
    step = 8
    low = lax.rem(lax.broadcasted_iota(jnp.int32, (pairs, step * 128), 1), 128) < proj
    for l in range(layers):
        wide = jnp.concatenate([right[l], right[l]], axis=1)
        wide = jnp.where(diagonal, jnp.concatenate([wide, wide], axis=0), 0.0)
        rr = jnp.concatenate(halves(wide), axis=0)
        lh, ll = (dot(dot(pick, m).astype(jnp.bfloat16), pick_t).astype(jnp.bfloat16) for m in halves(left[l]))
        lll = jnp.concatenate([lh, ll, lh], axis=1)
        x = jnp.concatenate([query[l, :, k * 128:(k + 1) * 128] for k in range(pairs)], axis=0)
        turned[l] = dot(jnp.concatenate([x, x], axis=1), rr)
        for q0 in range(0, rows, step):
            u = jnp.concatenate([turned[l, pl.ds(q, pairs, stride=rows), :] for q in range(q0, q0 + step)], axis=1)
            v = jnp.concatenate(
                [pltpu.roll(turned[l, pl.ds(q, pairs, stride=rows), :], proj, 1) for q in range(q0, q0 + step)], axis=1
            )
            wh, wl = halves(jnp.concatenate([jnp.where(low, u, v), jnp.where(low, v, u)], axis=0))
            z = dot(lll, jnp.concatenate([wh, wh, wl], axis=0))
            z = jnp.where(low, z[:half], z[half:])
            for n in range(step):
                mixed[l, pl.ds(q0 + n, pairs, stride=rows), :] = z[:, n * 128:(n + 1) * 128]
        for m in range(pairs):
            out[l, :, m * 128:(m + 1) * 128] = mixed[l, m * rows:(m + 1) * rows].astype(jnp.bfloat16)


def precondition(query, left, right):
    layers, rows, feat = query.shape
    scratch = pltpu.VMEM((layers, rows * feat // 128, 128), jnp.float32)
    return pl.pallas_call(
        precondition_kernel,
        out_shape=jax.ShapeDtypeStruct(query.shape, jnp.bfloat16),
        in_specs=[HBM] * 3,
        out_specs=VMEM,
        scratch_shapes=[
            pltpu.VMEM(query.shape, query.dtype),
            pltpu.VMEM(left.shape, left.dtype),
            pltpu.VMEM(right.shape, right.dtype),
            scratch,
            scratch,
            pltpu.SemaphoreType.DMA((3,)),
        ],
        compiler_params=pltpu.CompilerParams(vmem_limit_bytes=16 << 20),
        cost_estimate=pl.CostEstimate(flops=2 << 30, bytes_accessed=4 << 20, transcendentals=0),
        name="precondition",
    )(*(pltpu.with_memory_space_constraint(v, pltpu.HBM) for v in (query, left, right)))


def transpose_kernel(layer, train, out, buffer, sems):
    feat = train.shape[2]
    deep, rows, wide = buffer.shape
    steps = feat // wide

    def copy(n):
        return pltpu.make_async_copy(train.at[layer, :, pl.ds(n * wide, wide)], buffer.at[n % deep], sems.at[n % deep])

    for n in range(deep):
        copy(n).start()
    for n in range(steps):
        copy(n).wait()
        out[n * wide:(n + 1) * wide, :] = buffer[n % deep].T
        if n + deep < steps:
            copy(n + deep).start()


def transpose(layer, train):
    layers, rows, feat = train.shape
    wide, deep = 512, 8
    return pl.pallas_call(
        functools.partial(transpose_kernel, layer),
        out_shape=pltpu.VMEM((feat, rows), train.dtype),
        in_specs=[HBM],
        out_specs=VMEM,
        scratch_shapes=[pltpu.VMEM((deep, rows, wide), train.dtype), pltpu.SemaphoreType.DMA((deep,))],
        compiler_params=pltpu.CompilerParams(vmem_limit_bytes=16 << 20),
        cost_estimate=pl.CostEstimate(flops=2 << 30, bytes_accessed=8 << 20, transcendentals=0),
        name="transpose_%d" % layer,
    )(pltpu.with_memory_space_constraint(train, pltpu.HBM))


def score(turned, queries):
    total = None
    for l in range(len(turned)):
        rows = jnp.concatenate([q[l] for q in queries], axis=0)
        term = dot(rows, turned[l][...])
        total = term if total is None else total + term
    return total


def score_parts(turned, more, a, b, swapped, low, high):
    second = [q.at[1:] for q in (a, b, swapped)]
    return score((turned,), [a, b, swapped, low]) + score((more,), second + [high])


def chip_at(offset):
    row = lax.axis_index("row")
    chip, core = row // 2, lax.rem(row, 2)
    up, column = chip // 2, lax.rem(chip, 2)
    place = jnp.where(column == 0, up, 7 - up) - offset * (1 - 2 * core)
    place = lax.rem(place + 8, 8)
    return jnp.where(place < 4, 2 * place, 2 * (7 - place) + 1)


def foreign(offset):
    return chip_at(offset) // 4 != lax.axis_index("layer")


def put(out, at, offset, block):
    rows = block.shape[0] // 2
    core = lax.rem(lax.axis_index("row"), 2)
    if offset < 0:
        core = 1 - core
    start = (at - 4 * lax.axis_index("layer")) * 2 * rows
    out[pl.ds(pl.multiple_of(start + core * rows, rows), rows), :] = block[:rows]
    out[pl.ds(pl.multiple_of(start + (1 - core) * rows, rows), rows), :] = block[rows:]


def split(offset, ahead, behind, sent, kept):
    @pl.when(foreign(offset))
    def _():
        sent[...] = ahead[...]
        kept[...] = behind[...]

    @pl.when(jnp.logical_not(foreign(offset)))
    def _():
        sent[...] = behind[...]
        kept[...] = ahead[...]


def plain_kernel(turned, more, *refs):
    refs[-1][...] = score((turned, more), refs[:-1])


def second_kernel(turned, more, *refs):
    *queries, sent, kept, total = refs
    half = sent.shape[0]
    total[...] = score_parts(turned, more, *queries)
    split(2, total.at[:half], total.at[half:], sent, kept)


def third_kernel(turned, more, first, *refs):
    *queries, sent, kept, total = refs
    half = total.shape[0] // 2
    total[...] = score_parts(turned, more, *queries)
    split(1, first.at[:half], total.at[half:], sent.at[:half], kept.at[:half])
    split(3, total.at[:half], first.at[half:], sent.at[half:], kept.at[half:])


def fourth_kernel(turned, more, own, *refs):
    a, low0, low1, high0, high1, sent, kept, total = refs
    total[...] = score((turned,), [a, low0, low1]) + score((more,), [a.at[1:], high0, high1])
    split(4, total, own, sent, kept)


def block_call(kernel, name, rows, total, turned, operands):
    columns = turned[0].shape[1]
    block = jax.ShapeDtypeStruct((rows, columns), jnp.float32)
    return pl.pallas_call(
        kernel,
        out_shape=(block, block) if total else block,
        in_specs=[VMEM] * (2 + len(operands)),
        out_specs=(VMEM, VMEM) if total else VMEM,
        scratch_shapes=[pltpu.VMEM((total, columns), jnp.float32)] if total else [],
        compiler_params=pltpu.CompilerParams(vmem_limit_bytes=24 << 20),
        cost_estimate=pl.CostEstimate(flops=1 << 10, bytes_accessed=1 << 10, transcendentals=0),
        name=name,
    )(*turned, *operands)


def gather_kernel(kept2, got2, kept13, got13, out):
    half = kept2.shape[0]

    def place(offset, kept, got):
        block = kept[...] + got[...]

        @pl.when(foreign(offset))
        def _():
            put(out, chip_at(offset - 4), offset - 4, block)

        @pl.when(jnp.logical_not(foreign(offset)))
        def _():
            put(out, chip_at(offset), offset, block)

    place(2, kept2, got2)
    place(1, kept13.at[:half], got13.at[:half])
    place(3, kept13.at[half:], got13.at[half:])


def last_kernel(kept, got, table, out, block, sems):
    del table
    rows = kept.shape[0] // 2
    block[...] = kept[...] + got[...]
    at = jnp.where(foreign(4), chip_at(0), chip_at(4)) - 4 * lax.axis_index("layer")
    core = lax.rem(lax.axis_index("row"), 2)
    copies = []
    for n, c in enumerate((core, 1 - core)):
        start = pl.multiple_of((2 * at + c) * rows, rows)
        copies.append(pltpu.make_async_copy(block.at[n * rows:(n + 1) * rows], out.at[pl.ds(start, rows)], sems.at[n]))
    for copy in copies:
        copy.start()
    for copy in copies:
        copy.wait()


def finish(parts, rows, columns):
    (kept2, got2), (kept13, got13), (kept4, got4) = parts
    hbm = pl.BlockSpec(memory_space=pl.ANY)
    table = jax.ShapeDtypeStruct((rows, columns), jnp.float32)
    params = pltpu.CompilerParams(vmem_limit_bytes=8 << 20)
    most = pl.pallas_call(
        gather_kernel, out_shape=table, in_specs=[VMEM] * 4, out_specs=VMEM, compiler_params=params, name="gather_rows",
        cost_estimate=pl.CostEstimate(flops=60 << 30, bytes_accessed=1 << 20, transcendentals=0),
    )(kept2, got2, kept13, got13)
    return pl.pallas_call(
        last_kernel,
        out_shape=table,
        in_specs=[VMEM, VMEM, hbm],
        out_specs=hbm,
        scratch_shapes=[pltpu.VMEM(kept4.shape, jnp.float32), pltpu.SemaphoreType.DMA((2,))],
        input_output_aliases={2: 0},
        compiler_params=params,
        name="last_rows",
    )(kept4, got4, most)


def ring_order(chips):
    half = chips // 2
    return [2 * i for i in range(half)] + [2 * i + 1 for i in reversed(range(half))]


def ring_device(query_grads, train_grads, left_inverse, right_inverse):
    chips, groups, cores = 8, 2, 2
    order = ring_order(chips)
    flat = lambda layer, chip, core: (layer * chips + chip) * cores + core
    every = [(y, h, c) for y in range(groups) for h in range(chips) for c in range(cores)]
    step = lambda h, c: order[(order.index(h) + (1 - 2 * c)) % chips]
    swap = [(flat(y, h, c), flat(y, h, 1 - c)) for y, h, c in every]
    across = [(flat(y, h, c), flat(1 - y, h, c)) for y, h, c in every]
    around = [(flat(y, h, c), flat(y, step(h, c), c)) for y, h, c in every]
    send = lambda v, pairs: lax.ppermute(v, AXES, pairs)

    after = lax.optimization_barrier
    mine = precondition(query_grads, left_inverse, right_inverse)
    turned = [transpose(0, train_grads)]
    a, b = [mine, send(mine, around)], [send(mine, swap)]
    (b0, turned[0]) = after((b[0], turned[0]))
    turned.append(transpose(1, train_grads))
    b.append(send(b0, around))
    rows = 2 * mine.shape[1]
    zeroth = block_call(plain_kernel, "scores_0", rows, 0, turned, [a[0], b0])
    a.append(send(a[1], around))
    b[1], zeroth = after((b[1], zeroth))
    b.append(send(b[1], around))
    first = block_call(plain_kernel, "scores_1", 2 * rows, 0, turned, [a[1], b[1], send(a[1], swap), send(b[1], swap)])
    a.append(send(a[2], around))
    b[2], first = after((b[2], first))
    b.append(send(b[2], around))
    sent2, kept2 = block_call(second_kernel, "scores_2", rows, 2 * rows, turned, [a[2], b[2], send(a[2], swap), *(send(b[2][l:l + 1], swap) for l in range(2))])
    a[3], _ = after((a[3], sent2))
    a.append(send(a[3], around))
    got2 = send(sent2, across)
    b[3], _ = after((b[3], got2))
    sent3, kept3 = block_call(third_kernel, "scores_3", 2 * rows, 2 * rows, turned, [first, a[3], b[3], send(a[3], swap), *(send(b[3][l:l + 1], swap) for l in range(2))])
    a[4], _ = after((a[4], sent3))
    got3 = send(sent3, across)
    ends = [a[4], *(send(a[4][l:l + 1, 16 * n:16 * n + 16], swap) for l in range(2) for n in range(2))]
    sent4, kept4 = block_call(fourth_kernel, "scores_4", rows, rows, turned, [zeroth, *ends])
    pairs = [(kept2, got2), (kept3, got3), (kept4, send(sent4, across))]
    return finish(pairs, chips // groups * rows, turned[0].shape[1])


def on_device(query_grads, train_grads, left_inverse, right_inverse):
    layers, rows, feat = query_grads.shape
    proj = left_inverse.shape[1]
    square = query_grads.astype(jnp.float32).reshape(layers, rows, proj, proj)
    rotated = jnp.einsum(
        "lab,lqbc,lcd->lqad", left_inverse, square, right_inverse, precision=lax.Precision.HIGHEST
    )
    rotated = rotated.reshape(layers, rows, feat).astype(jnp.bfloat16)
    partial_value = jnp.einsum(
        "lqf,ltf->qt",
        lax.all_gather(rotated, "row", axis=1, tiled=True),
        train_grads,
        preferred_element_type=jnp.float32,
    )
    return lax.psum_scatter(partial_value, "layer", scatter_dimension=0, tiled=True)


def solution(mesh):
    placed = (
        P("layer", "row", None),
        P("layer", "row", None),
        P("layer", None, None),
        P("layer", None, None),
    )
    ring = mesh.shape["layer"] == 2 and mesh.shape["row"] == 16
    return jax.shard_map(
        ring_device if ring else on_device, mesh=mesh, in_specs=placed, out_specs=P("layer", "row"), check_vma=False
    )
```

```python
import functools

import jax
import jax.numpy as jnp
from jax import lax
from jax.experimental import pallas as pl
from jax.experimental.pallas import tpu as pltpu
from jax.sharding import PartitionSpec as P

AXES = ("layer", "row")
VMEM = pl.BlockSpec(memory_space=pltpu.VMEM)
HBM = pl.BlockSpec(memory_space=pl.ANY)


def halves(v):
    top = v.astype(jnp.bfloat16)
    return top, (v - top.astype(jnp.float32)).astype(jnp.bfloat16)


def dot(a, b):
    return jnp.dot(a, b, preferred_element_type=jnp.float32)


def precondition_first_kernel(query_hbm, left_hbm, right_hbm, out, query, left, right, *refs):
    *scratch, sems = refs
    copies = [
        pltpu.make_async_copy(src, dst, sems.at[n])
        for n, (src, dst) in enumerate(((left_hbm, left), (right_hbm, right), (query_hbm, query)))
    ]
    for copy in copies:
        copy.start()
    copies[0].wait()
    copies[1].wait()
    precondition_kernel(query, left, right, out, *scratch, arrived=copies[2].wait)


def precondition_kernel(query, left, right, out, turned, mixed, arrived=lambda: None):
    layers, rows, feat = query.shape
    proj = left.shape[1]
    half, pairs, stride = proj // 2, feat // 128, mixed.shape[1] // (feat // 128)
    i = lax.broadcasted_iota(jnp.int32, (2 * proj, 4 * proj), 0) // proj
    j = lax.broadcasted_iota(jnp.int32, (2 * proj, 4 * proj), 1) // (2 * proj)
    same = i == j
    i = lax.broadcasted_iota(jnp.int32, (proj, proj), 0)
    j = lax.broadcasted_iota(jnp.int32, (proj, proj), 1)
    pick = (j == 2 * lax.rem(i, half) + i // half).astype(jnp.bfloat16)
    pick_t = (i == 2 * lax.rem(j, half) + j // half).astype(jnp.bfloat16)
    rights, lefts = [], []
    for l in range(layers):
        wide = jnp.concatenate([right[l], right[l]], axis=1)
        wide = jnp.concatenate([wide, wide], axis=1)
        wide = jnp.where(same, jnp.concatenate([wide, wide], axis=0), 0.0)
        rights.append(jnp.concatenate(halves(wide), axis=0))
        high, low = halves(left[l])
        both = dot(pick, jnp.concatenate([high, low], axis=1)).astype(jnp.bfloat16)
        high, low = (dot(both[:, n:n + proj], pick_t).astype(jnp.bfloat16) for n in (0, proj))
        lefts.append(jnp.concatenate([high, low, high], axis=1))
    arrived()
    for l in range(layers):
        x = jnp.concatenate([query[l, :, k * 128:(k + 1) * 128] for k in range(pairs)], axis=0)
        y = dot(jnp.concatenate([x, x], axis=1), rights[l])
        for p in range(2):
            for k in range(pairs):
                turned[l, p, k * stride:k * stride + rows] = y[k * rows:(k + 1) * rows, p * 128:(p + 1) * 128]
    step = 8
    first = lax.rem(lax.broadcasted_iota(jnp.int32, (pairs, step * 128), 1), 128) < proj
    for l in range(layers):
        for q in range(0, rows, step):
            y = [
                jnp.concatenate([turned[l, p, pl.ds(q + n, pairs, stride=stride), :] for n in range(step)], axis=1)
                for p in range(2)
            ]
            high, low = halves(jnp.concatenate(y, axis=0))
            z = dot(lefts[l], jnp.concatenate([high, high, low], axis=0))
            z = jnp.where(first, z[:half], z[half:])
            for n in range(step):
                mixed[l, pl.ds(q + n, pairs, stride=stride), :] = z[:, n * 128:(n + 1) * 128]
        for m in range(pairs):
            out[l, :, m * 128:(m + 1) * 128] = mixed[l, m * stride:m * stride + rows].astype(jnp.bfloat16)


def precondition(query, left, right, first):
    layers, rows, feat = query.shape
    spread = (rows + 8) * feat // 128
    scratch = [pltpu.VMEM((layers, 2, spread, 128), jnp.float32), pltpu.VMEM((layers, spread, 128), jnp.float32)]
    operands = (query, left, right)
    if first:
        scratch = [pltpu.VMEM(v.shape, v.dtype) for v in operands] + scratch + [pltpu.SemaphoreType.DMA((3,))]
        operands = [pltpu.with_memory_space_constraint(v, pltpu.HBM) for v in operands]
    return pl.pallas_call(
        precondition_first_kernel if first else precondition_kernel,
        out_shape=jax.ShapeDtypeStruct(query.shape, jnp.bfloat16),
        in_specs=[HBM if first else VMEM] * 3,
        out_specs=VMEM,
        scratch_shapes=scratch,
        compiler_params=pltpu.CompilerParams(vmem_limit_bytes=16 << 20),
        cost_estimate=pl.CostEstimate(flops=2 << 30, bytes_accessed=4 << 20, transcendentals=0),
        name="precondition_0" if first else "precondition_1",
    )(*operands)


def transpose_kernel(layer, train, out, buffer, sems):
    feat = train.shape[2]
    deep, rows, wide = buffer.shape
    steps = feat // wide

    def copy(n):
        return pltpu.make_async_copy(train.at[layer, :, pl.ds(n * wide, wide)], buffer.at[n % deep], sems.at[n % deep])

    for n in range(deep):
        copy(n).start()
    for n in range(steps):
        copy(n).wait()
        out[n * wide:(n + 1) * wide, :] = buffer[n % deep].T
        if n + deep < steps:
            copy(n + deep).start()


def transpose(layer, train):
    layers, rows, feat = train.shape
    wide, deep = 512, 8
    return pl.pallas_call(
        functools.partial(transpose_kernel, layer),
        out_shape=pltpu.VMEM((feat, rows), train.dtype),
        in_specs=[HBM],
        out_specs=VMEM,
        scratch_shapes=[pltpu.VMEM((deep, rows, wide), train.dtype), pltpu.SemaphoreType.DMA((deep,))],
        compiler_params=pltpu.CompilerParams(vmem_limit_bytes=16 << 20),
        cost_estimate=pl.CostEstimate(flops=2 << 30, bytes_accessed=8 << 20, transcendentals=0),
        name="transpose_%d" % layer,
    )(pltpu.with_memory_space_constraint(train, pltpu.HBM))


def score(turned, queries):
    total = None
    for l in range(len(turned)):
        rows = jnp.concatenate([q[l] for q in queries], axis=0)
        term = dot(rows, turned[l][...])
        total = term if total is None else total + term
    return total


def score_parts(turned, more, a, b, swapped, low, high):
    second = [q.at[1:] for q in (a, b, swapped)]
    return score((turned,), [a, b, swapped, low]) + score((more,), second + [high])


def chip_at(offset):
    row = lax.axis_index("row")
    chip, core = row // 2, lax.rem(row, 2)
    up, column = chip // 2, lax.rem(chip, 2)
    place = jnp.where(column == 0, up, 7 - up) - offset * (1 - 2 * core)
    place = lax.rem(place + 8, 8)
    return jnp.where(place < 4, 2 * place, 2 * (7 - place) + 1)


def foreign(offset):
    return chip_at(offset) // 4 != lax.axis_index("layer")


def put(out, at, offset, block):
    rows = block.shape[0] // 2
    core = lax.rem(lax.axis_index("row"), 2)
    if offset < 0:
        core = 1 - core
    start = (at - 4 * lax.axis_index("layer")) * 2 * rows
    out[pl.ds(pl.multiple_of(start + core * rows, rows), rows), :] = block[:rows]
    out[pl.ds(pl.multiple_of(start + (1 - core) * rows, rows), rows), :] = block[rows:]


def split(offset, ahead, behind, sent, kept):
    @pl.when(foreign(offset))
    def _():
        sent[...] = ahead[...].astype(sent.dtype)
        kept[...] = behind[...]

    @pl.when(jnp.logical_not(foreign(offset)))
    def _():
        sent[...] = behind[...].astype(sent.dtype)
        kept[...] = ahead[...]


def plain_kernel(turned, more, *refs):
    refs[-1][...] = score((turned, more), refs[:-1])


def second_kernel(turned, more, *refs):
    refs[-1][...] = score_parts(turned, more, *refs[:-1])


def third_kernel(turned, more, first, second, *refs):
    *queries, sent, kept, total = refs
    half = total.shape[0] // 2
    total[...] = score_parts(turned, more, *queries)
    at = [pl.ds(n * half, half) for n in range(3)]
    split(1, first.at[at[0]], total.at[at[1]], sent.at[at[0]], kept.at[at[0]])
    split(2, second.at[at[0]], second.at[at[1]], sent.at[at[1]], kept.at[at[1]])
    split(3, total.at[at[0]], first.at[at[1]], sent.at[at[2]], kept.at[at[2]])


def fourth_kernel(turned, more, own, *refs):
    a, low0, low1, high0, high1, sent, kept, total = refs
    total[...] = score((turned,), [a, low0, low1]) + score((more,), [a.at[1:], high0, high1])
    split(4, total, own, sent, kept)


def block_call(kernel, name, rows, total, turned, operands, kind=jnp.float32):
    columns = turned[0].shape[1]
    block = jax.ShapeDtypeStruct((rows, columns), jnp.float32)
    return pl.pallas_call(
        kernel,
        out_shape=(jax.ShapeDtypeStruct(block.shape, kind), block) if total else block,
        in_specs=[VMEM] * (2 + len(operands)),
        out_specs=(VMEM, VMEM) if total else VMEM,
        scratch_shapes=[pltpu.VMEM((total, columns), jnp.float32)] if total else [],
        compiler_params=pltpu.CompilerParams(vmem_limit_bytes=24 << 20),
        cost_estimate=pl.CostEstimate(flops=1 << 10, bytes_accessed=1 << 10, transcendentals=0),
        name=name,
    )(*turned, *operands)


def gather_kernel(kept, got, out):
    rows = kept.shape[0] // 3
    for n in range(3):
        offset = n + 1
        block = kept[n * rows:(n + 1) * rows] + got[n * rows:(n + 1) * rows].astype(kept.dtype)

        @pl.when(foreign(offset))
        def _():
            put(out, chip_at(offset - 4), offset - 4, block)

        @pl.when(jnp.logical_not(foreign(offset)))
        def _():
            put(out, chip_at(offset), offset, block)


def last_kernel(kept, got, table, out, block, sems):
    del table
    rows = kept.shape[0] // 2
    block[...] = kept[...] + got[...].astype(kept.dtype)
    at = jnp.where(foreign(4), chip_at(0), chip_at(4)) - 4 * lax.axis_index("layer")
    core = lax.rem(lax.axis_index("row"), 2)
    copies = []
    for n, c in enumerate((core, 1 - core)):
        start = pl.multiple_of((2 * at + c) * rows, rows)
        copies.append(pltpu.make_async_copy(block.at[n * rows:(n + 1) * rows], out.at[pl.ds(start, rows)], sems.at[n]))
    for copy in copies:
        copy.start()
    for copy in copies:
        copy.wait()


def finish(kept, got, kept4, got4, rows, columns):
    hbm = pl.BlockSpec(memory_space=pl.ANY)
    table = jax.ShapeDtypeStruct((rows, columns), jnp.float32)
    params = pltpu.CompilerParams(vmem_limit_bytes=8 << 20)
    most = pl.pallas_call(
        gather_kernel, out_shape=table, in_specs=[VMEM] * 2, out_specs=VMEM, compiler_params=params, name="gather_rows",
        cost_estimate=pl.CostEstimate(flops=60 << 30, bytes_accessed=1 << 20, transcendentals=0),
    )(kept, got)
    return pl.pallas_call(
        last_kernel,
        out_shape=table,
        in_specs=[VMEM, VMEM, hbm],
        out_specs=hbm,
        scratch_shapes=[pltpu.VMEM(kept4.shape, jnp.float32), pltpu.SemaphoreType.DMA((2,))],
        input_output_aliases={2: 0},
        compiler_params=params,
        name="last_rows",
    )(kept4, got4, most)


def ring_order(chips):
    half = chips // 2
    return [2 * i for i in range(half)] + [2 * i + 1 for i in reversed(range(half))]


def ring_device(query_grads, train_grads, left_inverse, right_inverse):
    chips, groups, cores = 8, 2, 2
    order = ring_order(chips)
    flat = lambda layer, chip, core: (layer * chips + chip) * cores + core
    every = [(y, h, c) for y in range(groups) for h in range(chips) for c in range(cores)]
    step = lambda h, c: order[(order.index(h) + (1 - 2 * c)) % chips]
    swap = [(flat(y, h, c), flat(y, h, 1 - c)) for y, h, c in every]
    across = [(flat(y, h, c), flat(1 - y, h, c)) for y, h, c in every]
    around = [(flat(y, h, c), flat(y, step(h, c), c)) for y, h, c in every]
    send = lambda v, pairs: lax.ppermute(v, AXES, pairs)

    after = lax.optimization_barrier
    arrived = [send(query_grads, around), send(send(query_grads, swap), around)]
    mine = precondition(query_grads, left_inverse, right_inverse, True)
    a, b = [mine], [send(mine, swap)]
    turned = [transpose(l, train_grads) for l in range(2)]
    arrived[0], *turned = after((arrived[0], *turned))
    a.append(precondition(arrived[0], left_inverse, right_inverse, False))
    b.append(precondition(arrived[1], left_inverse, right_inverse, False))
    rows = 2 * mine.shape[1]
    zeroth = block_call(plain_kernel, "scores_0", rows, 0, turned, [a[0], b[0]])
    a.append(send(a[1], around))
    b.append(send(b[1], around))
    first = block_call(plain_kernel, "scores_1", 2 * rows, 0, turned, [a[1], b[1], send(a[1], swap), send(b[1], swap)])
    a.append(send(a[2], around))
    b[2], first, _ = after((b[2], first, mine))
    b.append(send(b[2], around))
    second = block_call(second_kernel, "scores_2", 2 * rows, 0, turned, [a[2], b[2], send(a[2], swap), *(send(b[2][l:l + 1], swap) for l in range(2))])
    a[3], second, zeroth = after((a[3], second, zeroth))
    a.append(send(a[3], around))
    queries = [a[3], b[3], send(a[3], swap), *(send(b[3][l:l + 1], swap) for l in range(2))]
    sent, kept = block_call(third_kernel, "scores_3", 3 * rows, 2 * rows, turned, [first, second] + queries, jnp.bfloat16)
    a[4], _ = after((a[4], sent))
    got = send(sent, across)
    end = [a[4], *(send(a[4][l:l + 1, 16 * n:16 * n + 16], swap) for l in range(2) for n in range(2))]
    sent4, kept4 = block_call(fourth_kernel, "scores_4", rows, rows, turned, [zeroth, *end], jnp.bfloat16)
    return finish(kept, got, kept4, send(sent4, across), chips // groups * rows, turned[0].shape[1])


def on_device(query_grads, train_grads, left_inverse, right_inverse):
    layers, rows, feat = query_grads.shape
    proj = left_inverse.shape[1]
    square = query_grads.astype(jnp.float32).reshape(layers, rows, proj, proj)
    rotated = jnp.einsum(
        "lab,lqbc,lcd->lqad", left_inverse, square, right_inverse, precision=lax.Precision.HIGHEST
    )
    rotated = rotated.reshape(layers, rows, feat).astype(jnp.bfloat16)
    partial_value = jnp.einsum(
        "lqf,ltf->qt",
        lax.all_gather(rotated, "row", axis=1, tiled=True),
        train_grads,
        preferred_element_type=jnp.float32,
    )
    return lax.psum_scatter(partial_value, "layer", scatter_dimension=0, tiled=True)


def solution(mesh):
    placed = (
        P("layer", "row", None),
        P("layer", "row", None),
        P("layer", None, None),
        P("layer", None, None),
    )
    ring = mesh.shape["layer"] == 2 and mesh.shape["row"] == 16
    return jax.shard_map(
        ring_device if ring else on_device, mesh=mesh, in_specs=placed, out_specs=P("layer", "row"), check_vma=False
    )
```

```python
import functools

import jax
import jax.numpy as jnp
from jax import lax
from jax.experimental import pallas as pl
from jax.experimental.pallas import tpu as pltpu
from jax.sharding import PartitionSpec as P

AXES = ("layer", "row")
VMEM = pl.BlockSpec(memory_space=pltpu.VMEM)
HBM = pl.BlockSpec(memory_space=pl.ANY)


def halves(v):
    top = v.astype(jnp.bfloat16)
    return top, (v - top.astype(jnp.float32)).astype(jnp.bfloat16)


def dot(a, b):
    return jnp.dot(a, b, preferred_element_type=jnp.float32)


def precondition_first_kernel(query_hbm, left_hbm, right_hbm, out, query, left, right, *refs):
    *scratch, sems = refs
    copies = [
        pltpu.make_async_copy(src, dst, sems.at[n])
        for n, (src, dst) in enumerate(((left_hbm, left), (right_hbm, right), (query_hbm, query)))
    ]
    for copy in copies:
        copy.start()
    copies[0].wait()
    copies[1].wait()
    precondition_kernel(query, left, right, out, *scratch, arrived=copies[2].wait)


def precondition_kernel(query, left, right, out, turned, mixed, arrived=lambda: None):
    layers, rows, feat = query.shape
    proj = left.shape[1]
    half, pairs, stride = proj // 2, feat // 128, mixed.shape[1] // (feat // 128)
    i = lax.broadcasted_iota(jnp.int32, (2 * proj, 4 * proj), 0) // proj
    j = lax.broadcasted_iota(jnp.int32, (2 * proj, 4 * proj), 1) // (2 * proj)
    same = i == j
    i = lax.broadcasted_iota(jnp.int32, (proj, proj), 0)
    j = lax.broadcasted_iota(jnp.int32, (proj, proj), 1)
    pick = (j == 2 * lax.rem(i, half) + i // half).astype(jnp.bfloat16)
    pick_t = (i == 2 * lax.rem(j, half) + j // half).astype(jnp.bfloat16)
    rights, lefts = [], []
    for l in range(layers):
        wide = jnp.concatenate([right[l], right[l]], axis=1)
        wide = jnp.concatenate([wide, wide], axis=1)
        wide = jnp.where(same, jnp.concatenate([wide, wide], axis=0), 0.0)
        rights.append(jnp.concatenate(halves(wide), axis=0))
        high, low = halves(left[l])
        both = dot(pick, jnp.concatenate([high, low], axis=1)).astype(jnp.bfloat16)
        high, low = (dot(both[:, n:n + proj], pick_t).astype(jnp.bfloat16) for n in (0, proj))
        lefts.append(jnp.concatenate([high, low, high], axis=1))
    arrived()
    for l in range(layers):
        x = jnp.concatenate([query[l, :, k * 128:(k + 1) * 128] for k in range(pairs)], axis=0)
        y = dot(jnp.concatenate([x, x], axis=1), rights[l])
        for p in range(2):
            for k in range(pairs):
                turned[l, p, k * stride:k * stride + rows] = y[k * rows:(k + 1) * rows, p * 128:(p + 1) * 128]
    step = 8
    first = lax.rem(lax.broadcasted_iota(jnp.int32, (pairs, step * 128), 1), 128) < proj
    for l in range(layers):
        for q in range(0, rows, step):
            y = [
                jnp.concatenate([turned[l, p, pl.ds(q + n, pairs, stride=stride), :] for n in range(step)], axis=1)
                for p in range(2)
            ]
            high, low = halves(jnp.concatenate(y, axis=0))
            z = dot(lefts[l], jnp.concatenate([high, high, low], axis=0))
            z = jnp.where(first, z[:half], z[half:])
            for n in range(step):
                mixed[l, pl.ds(q + n, pairs, stride=stride), :] = z[:, n * 128:(n + 1) * 128]
        for m in range(pairs):
            out[l, :, m * 128:(m + 1) * 128] = mixed[l, m * stride:m * stride + rows].astype(jnp.bfloat16)


def precondition(query, left, right, first):
    layers, rows, feat = query.shape
    spread = (rows + 8) * feat // 128
    scratch = [pltpu.VMEM((layers, 2, spread, 128), jnp.float32), pltpu.VMEM((layers, spread, 128), jnp.float32)]
    operands = (query, left, right)
    if first:
        scratch = [pltpu.VMEM(v.shape, v.dtype) for v in operands] + scratch + [pltpu.SemaphoreType.DMA((3,))]
        operands = [pltpu.with_memory_space_constraint(v, pltpu.HBM) for v in operands]
    return pl.pallas_call(
        precondition_first_kernel if first else precondition_kernel,
        out_shape=jax.ShapeDtypeStruct(query.shape, jnp.bfloat16),
        in_specs=[HBM if first else VMEM] * 3,
        out_specs=VMEM,
        scratch_shapes=scratch,
        compiler_params=pltpu.CompilerParams(vmem_limit_bytes=16 << 20),
        cost_estimate=pl.CostEstimate(flops=2 << 30, bytes_accessed=4 << 20, transcendentals=0),
        name="precondition_0" if first else "precondition_1",
    )(*operands)


def transpose_kernel(layer, train, out, buffer, sems):
    feat = train.shape[2]
    deep, rows, wide = buffer.shape
    steps = feat // wide

    def copy(n):
        return pltpu.make_async_copy(train.at[layer, :, pl.ds(n * wide, wide)], buffer.at[n % deep], sems.at[n % deep])

    for n in range(deep):
        copy(n).start()
    for n in range(steps):
        copy(n).wait()
        out[n * wide:(n + 1) * wide, :] = buffer[n % deep].T
        if n + deep < steps:
            copy(n + deep).start()


def transpose(layer, train):
    layers, rows, feat = train.shape
    wide, deep = 512, 8
    return pl.pallas_call(
        functools.partial(transpose_kernel, layer),
        out_shape=pltpu.VMEM((feat, rows), train.dtype),
        in_specs=[HBM],
        out_specs=VMEM,
        scratch_shapes=[pltpu.VMEM((deep, rows, wide), train.dtype), pltpu.SemaphoreType.DMA((deep,))],
        compiler_params=pltpu.CompilerParams(vmem_limit_bytes=16 << 20),
        cost_estimate=pl.CostEstimate(flops=2 << 30, bytes_accessed=8 << 20, transcendentals=0),
        name="transpose_%d" % layer,
    )(pltpu.with_memory_space_constraint(train, pltpu.HBM))


def layer_score(turned, rows):
    rows = [row[...] for row in rows]
    count = sum(row.shape[0] for row in rows)
    rows = rows * max(1, 128 // count)
    return dot(jnp.concatenate(rows, axis=0), turned[...])[:count]


def pieces(unit, layer):
    if not isinstance(unit, (list, tuple)):
        return [unit.at[layer]]
    half = len(unit) // 2
    return [piece.at[0] for piece in unit[layer * half:(layer + 1) * half]]


def score(turned, more, units):
    return sum(
        layer_score(t, [piece for unit in units for piece in pieces(unit, layer)])
        for layer, t in enumerate((turned, more))
    )


def chip_at(offset):
    row = lax.axis_index("row")
    chip, core = row // 2, lax.rem(row, 2)
    up, column = chip // 2, lax.rem(chip, 2)
    place = jnp.where(column == 0, up, 7 - up) - offset * (1 - 2 * core)
    place = lax.rem(place + 8, 8)
    return jnp.where(place < 4, 2 * place, 2 * (7 - place) + 1)


def foreign(offset):
    return chip_at(offset) // 4 != lax.axis_index("layer")


def put(out, at, offset, block):
    rows = block.shape[0] // 2
    core = lax.rem(lax.axis_index("row"), 2)
    if offset < 0:
        core = 1 - core
    start = (at - 4 * lax.axis_index("layer")) * 2 * rows
    out[pl.ds(pl.multiple_of(start + core * rows, rows), rows), :] = block[:rows]
    out[pl.ds(pl.multiple_of(start + (1 - core) * rows, rows), rows), :] = block[rows:]


def split(offset, ahead, behind, sent, kept):
    @pl.when(foreign(offset))
    def _():
        sent[...] = ahead[...].astype(sent.dtype)
        kept[...] = behind[...]

    @pl.when(jnp.logical_not(foreign(offset)))
    def _():
        sent[...] = behind[...].astype(sent.dtype)
        kept[...] = ahead[...]


def plain_kernel(turned, more, *refs):
    refs[-1][...] = score(turned, more, refs[:-1])


def second_kernel(turned, more, own, *refs):
    *queries, sent, kept, total = refs
    half = kept.shape[0]
    total[...] = score(turned, more, [*queries[:3], queries[3:]])
    split(2, total.at[:half], total.at[half:], sent.at[:half], kept)
    sent[half:] = own[...].astype(sent.dtype)


def third_kernel(turned, more, first, *refs):
    *queries, sent, kept, total = refs
    half = total.shape[0] // 2
    total[...] = score(turned, more, [*queries[:3], queries[3:]])
    split(1, first.at[:half], total.at[half:], sent.at[:half], kept.at[:half])
    split(3, total.at[:half], first.at[half:], sent.at[half:2 * half], kept.at[half:])


def opening_kernel(turned, *refs):
    unit, *swapped, out = refs
    out[...] = layer_score(turned, [unit.at[0]] + [ref.at[0] for ref in swapped])


def second_layer(turned, opening, unit, swapped):
    return opening[...] + layer_score(turned, [unit.at[1]] + [ref.at[0] for ref in swapped])


def fourth_kernel(turned, opening, *refs):
    unit, *swapped, sent = refs

    @pl.when(foreign(4))
    def _():
        sent[...] = second_layer(turned, opening, unit, swapped).astype(sent.dtype)

    @pl.when(jnp.logical_not(foreign(4)))
    def _():
        sent[...] = jnp.zeros_like(sent)


def fifth_kernel(turned, opening, *refs):
    unit, *swapped, kept = refs

    @pl.when(jnp.logical_not(foreign(4)))
    def _():
        kept[...] = second_layer(turned, opening, unit, swapped)


def block_call(kernel, name, rows, total, turned, operands, kind=jnp.float32, sent=0):
    columns = turned[0].shape[1]
    block = jax.ShapeDtypeStruct((rows, columns), jnp.float32)
    one = total is None
    return pl.pallas_call(
        kernel,
        out_shape=(jax.ShapeDtypeStruct((max(rows, sent), columns), kind), block) if not one else jax.ShapeDtypeStruct(block.shape, kind),
        in_specs=[VMEM] * (len(turned) + len(operands)),
        out_specs=VMEM if one else (VMEM, VMEM),
        scratch_shapes=[pltpu.VMEM((total, columns), jnp.float32)] if total else [],
        compiler_params=pltpu.CompilerParams(vmem_limit_bytes=24 << 20),
        cost_estimate=pl.CostEstimate(flops=1 << 10, bytes_accessed=1 << 10, transcendentals=0),
        name=name,
    )(*turned, *operands)


def gather_kernel(kept2, got2, kept13, got13, own, out):
    rows = kept2.shape[0]
    low, high = pl.ds(0, rows), pl.ds(rows, rows)
    for offset, kept, got in (
        (2, kept2, got2.at[low]),
        (1, kept13.at[low], got13.at[low]),
        (3, kept13.at[high], got13.at[high]),
    ):
        block = kept[...] + got[...].astype(kept.dtype)

        @pl.when(foreign(offset))
        def _():
            put(out, chip_at(offset - 4), offset - 4, block)

        @pl.when(jnp.logical_not(foreign(offset)))
        def _():
            put(out, chip_at(offset), offset, block)

    @pl.when(foreign(4))
    def _():
        put(out, chip_at(0), 0, own[...] + got2[high].astype(own.dtype))


def last_kernel(kept, got, table, out, block, sems):
    del table

    @pl.when(jnp.logical_not(foreign(4)))
    def _():
        rows = kept.shape[0] // 2
        block[...] = kept[...] + got[...].astype(kept.dtype)
        at = chip_at(4) - 4 * lax.axis_index("layer")
        core = lax.rem(lax.axis_index("row"), 2)
        copies = []
        for n, c in enumerate((core, 1 - core)):
            start = pl.multiple_of((2 * at + c) * rows, rows)
            copies.append(
                pltpu.make_async_copy(block.at[n * rows:(n + 1) * rows], out.at[pl.ds(start, rows)], sems.at[n])
            )
        for copy in copies:
            copy.start()
        for copy in copies:
            copy.wait()


def finish(most, last, rows, columns):
    table = jax.ShapeDtypeStruct((rows, columns), jnp.float32)
    params = pltpu.CompilerParams(vmem_limit_bytes=8 << 20)
    gathered = pl.pallas_call(
        gather_kernel,
        out_shape=table,
        in_specs=[VMEM] * 5,
        out_specs=VMEM,
        compiler_params=params,
        cost_estimate=pl.CostEstimate(flops=60 << 30, bytes_accessed=1 << 20, transcendentals=0),
        name="gather_rows",
    )(*most)
    return pl.pallas_call(
        last_kernel,
        out_shape=table,
        in_specs=[VMEM, VMEM, HBM],
        out_specs=HBM,
        scratch_shapes=[pltpu.VMEM(last[0].shape, jnp.float32), pltpu.SemaphoreType.DMA((2,))],
        input_output_aliases={2: 0},
        compiler_params=params,
        name="last_rows",
    )(*last, gathered)


def ring_order(chips):
    half = chips // 2
    return [2 * i for i in range(half)] + [2 * i + 1 for i in reversed(range(half))]


def ring_device(query_grads, train_grads, left_inverse, right_inverse):
    chips, groups, cores = 8, 2, 2
    order = ring_order(chips)
    flat = lambda layer, chip, core: (layer * chips + chip) * cores + core
    every = [(y, h, c) for y in range(groups) for h in range(chips) for c in range(cores)]
    step = lambda h, c: order[(order.index(h) + (1 - 2 * c)) % chips]
    swap = [(flat(y, h, c), flat(y, h, 1 - c)) for y, h, c in every]
    across = [(flat(y, h, c), flat(1 - y, h, c)) for y, h, c in every]
    around = [(flat(y, h, c), flat(y, step(h, c), c)) for y, h, c in every]
    send = lambda v, pairs: lax.ppermute(v, AXES, pairs)

    after = lax.optimization_barrier
    def quarters(unit):
        layers, held, feat = unit.shape
        half = held // 2
        return [send(unit[l:l + 1, n:n + half], swap) for l in range(layers) for n in (0, half)]

    halves_of = lambda unit: [send(unit[l:l + 1], swap) for l in range(unit.shape[0])]

    arrived = [send(query_grads, around), send(send(query_grads, swap), around)]
    mine = precondition(query_grads, left_inverse, right_inverse, True)
    a, b = [mine], [send(mine, swap)]
    turned = [transpose(l, train_grads) for l in range(2)]
    arrived[0], *turned = after((arrived[0], *turned))
    a.append(precondition(arrived[0], left_inverse, right_inverse, False))
    b.append(precondition(arrived[1], left_inverse, right_inverse, False))
    rows = 2 * mine.shape[1]
    zeroth = block_call(plain_kernel, "scores_0", rows, None, turned, [a[0], b[0]])
    a.append(send(a[1], around))
    b.append(send(b[1], around))
    first = block_call(plain_kernel, "scores_1", 2 * rows, None, turned, [a[1], b[1], send(a[1], swap), send(b[1], swap)])
    a.append(send(a[2], around))
    b[2], first, _ = after((b[2], first, mine))
    b.append(send(b[2], around))
    queries = [a[2], b[2], send(a[2], swap), *halves_of(b[2])]
    sent2, kept2 = block_call(second_kernel, "scores_2", rows, 2 * rows, turned, [zeroth] + queries, jnp.bfloat16, 2 * rows)
    a[3], _ = after((a[3], sent2))
    a.append(send(a[3], around))
    got2 = send(sent2, across)
    b[3], got2 = after((b[3], got2))
    queries = [a[3], b[3], send(a[3], swap), *halves_of(b[3])]
    sent, kept = block_call(third_kernel, "scores_3", 2 * rows, 2 * rows, turned, [first] + queries, jnp.bfloat16, 2 * rows + 32)
    got = send(sent, across)
    a[4], _ = after((a[4], sent))
    swapped = quarters(a[4])
    opening = block_call(opening_kernel, "scores_4", rows, None, turned[:1], [a[4], *swapped[:2]])
    sent4 = block_call(fourth_kernel, "scores_5", rows, None, turned[1:], [opening, a[4], *swapped[2:]], jnp.bfloat16)
    got4 = send(sent4, across)
    kept4 = block_call(fifth_kernel, "scores_6", rows, None, turned[1:], [opening, a[4], *swapped[2:]])
    return finish((kept2, got2, kept, got, zeroth), (kept4, got4), chips // groups * rows, turned[0].shape[1])


def on_device(query_grads, train_grads, left_inverse, right_inverse):
    layers, rows, feat = query_grads.shape
    proj = left_inverse.shape[1]
    square = query_grads.astype(jnp.float32).reshape(layers, rows, proj, proj)
    rotated = jnp.einsum(
        "lab,lqbc,lcd->lqad", left_inverse, square, right_inverse, precision=lax.Precision.HIGHEST
    )
    rotated = rotated.reshape(layers, rows, feat).astype(jnp.bfloat16)
    partial_value = jnp.einsum(
        "lqf,ltf->qt",
        lax.all_gather(rotated, "row", axis=1, tiled=True),
        train_grads,
        preferred_element_type=jnp.float32,
    )
    return lax.psum_scatter(partial_value, "layer", scatter_dimension=0, tiled=True)


def solution(mesh):
    placed = (
        P("layer", "row", None),
        P("layer", "row", None),
        P("layer", None, None),
        P("layer", None, None),
    )
    ring = mesh.shape["layer"] == 2 and mesh.shape["row"] == 16
    return jax.shard_map(
        ring_device if ring else on_device, mesh=mesh, in_specs=placed, out_specs=P("layer", "row"), check_vma=False
    )
```

```python
import functools

import jax
import jax.numpy as jnp
from jax import lax
from jax.experimental import pallas as pl
from jax.experimental.pallas import tpu as pltpu
from jax.sharding import PartitionSpec as P

AXES = ("layer", "row")
VMEM = pl.BlockSpec(memory_space=pltpu.VMEM)
HBM = pl.BlockSpec(memory_space=pl.ANY)


def halves(v):
    top = v.astype(jnp.bfloat16)
    return top, (v - top.astype(jnp.float32)).astype(jnp.bfloat16)


def dot(a, b):
    return jnp.dot(a, b, preferred_element_type=jnp.float32)


def precondition_first_kernel(query_hbm, left_hbm, right_hbm, out, query, left, right, *refs):
    *scratch, sems = refs
    copies = [
        pltpu.make_async_copy(src, dst, sems.at[n])
        for n, (src, dst) in enumerate(((left_hbm, left), (right_hbm, right), (query_hbm, query)))
    ]
    for copy in copies:
        copy.start()
    copies[0].wait()
    copies[1].wait()
    precondition_kernel(query, left, right, out, *scratch, arrived=copies[2].wait)


def precondition_kernel(query, left, right, out, turned, mixed, arrived=lambda: None):
    layers, rows, feat = query.shape
    proj = left.shape[1]
    half, pairs, stride = proj // 2, feat // 128, mixed.shape[1] // (feat // 128)
    i = lax.broadcasted_iota(jnp.int32, (2 * proj, 4 * proj), 0) // proj
    j = lax.broadcasted_iota(jnp.int32, (2 * proj, 4 * proj), 1) // (2 * proj)
    same = i == j
    i = lax.broadcasted_iota(jnp.int32, (proj, proj), 0)
    j = lax.broadcasted_iota(jnp.int32, (proj, proj), 1)
    pick = (j == 2 * lax.rem(i, half) + i // half).astype(jnp.bfloat16)
    pick_t = (i == 2 * lax.rem(j, half) + j // half).astype(jnp.bfloat16)
    rights, lefts = [], []
    for l in range(layers):
        wide = jnp.concatenate([right[l], right[l]], axis=1)
        wide = jnp.concatenate([wide, wide], axis=1)
        wide = jnp.where(same, jnp.concatenate([wide, wide], axis=0), 0.0)
        rights.append(jnp.concatenate(halves(wide), axis=0))
        high, low = halves(left[l])
        both = dot(pick, jnp.concatenate([high, low], axis=1)).astype(jnp.bfloat16)
        high, low = (dot(both[:, n:n + proj], pick_t).astype(jnp.bfloat16) for n in (0, proj))
        lefts.append(jnp.concatenate([high, low, high], axis=1))
    arrived()
    for l in range(layers):
        x = jnp.concatenate([query[l, :, k * 128:(k + 1) * 128] for k in range(pairs)], axis=0)
        y = dot(jnp.concatenate([x, x], axis=1), rights[l])
        for p in range(2):
            for k in range(pairs):
                turned[l, p, k * stride:k * stride + rows] = y[k * rows:(k + 1) * rows, p * 128:(p + 1) * 128]
    step = 8
    first = lax.rem(lax.broadcasted_iota(jnp.int32, (pairs, step * 128), 1), 128) < proj
    for l in range(layers):
        for q in range(0, rows, step):
            y = [
                jnp.concatenate([turned[l, p, pl.ds(q + n, pairs, stride=stride), :] for n in range(step)], axis=1)
                for p in range(2)
            ]
            high, low = halves(jnp.concatenate(y, axis=0))
            z = dot(lefts[l], jnp.concatenate([high, high, low], axis=0))
            z = jnp.where(first, z[:half], z[half:])
            for n in range(step):
                mixed[l, pl.ds(q + n, pairs, stride=stride), :] = z[:, n * 128:(n + 1) * 128]
        for m in range(pairs):
            out[l, :, m * 128:(m + 1) * 128] = mixed[l, m * stride:m * stride + rows].astype(jnp.bfloat16)


def precondition(query, left, right, first):
    layers, rows, feat = query.shape
    spread = (rows + 8) * feat // 128
    scratch = [pltpu.VMEM((layers, 2, spread, 128), jnp.float32), pltpu.VMEM((layers, spread, 128), jnp.float32)]
    operands = (query, left, right)
    if first:
        scratch = [pltpu.VMEM(v.shape, v.dtype) for v in operands] + scratch + [pltpu.SemaphoreType.DMA((3,))]
        operands = [pltpu.with_memory_space_constraint(v, pltpu.HBM) for v in operands]
    return pl.pallas_call(
        precondition_first_kernel if first else precondition_kernel,
        out_shape=jax.ShapeDtypeStruct(query.shape, jnp.bfloat16),
        in_specs=[HBM if first else VMEM] * 3,
        out_specs=VMEM,
        scratch_shapes=scratch,
        compiler_params=pltpu.CompilerParams(vmem_limit_bytes=16 << 20),
        cost_estimate=pl.CostEstimate(flops=2 << 30, bytes_accessed=4 << 20, transcendentals=0),
        name="precondition_0" if first else "precondition_1",
    )(*operands)


def transpose_kernel(layer, train, out, buffer, sems):
    feat = train.shape[2]
    deep, rows, wide = buffer.shape
    steps = feat // wide

    def copy(n):
        return pltpu.make_async_copy(train.at[layer, :, pl.ds(n * wide, wide)], buffer.at[n % deep], sems.at[n % deep])

    for n in range(deep):
        copy(n).start()
    for n in range(steps):
        copy(n).wait()
        out[n * wide:(n + 1) * wide, :] = buffer[n % deep].T
        if n + deep < steps:
            copy(n + deep).start()


def transpose(layer, train):
    layers, rows, feat = train.shape
    wide, deep = 512, 8
    return pl.pallas_call(
        functools.partial(transpose_kernel, layer),
        out_shape=pltpu.VMEM((feat, rows), train.dtype),
        in_specs=[HBM],
        out_specs=VMEM,
        scratch_shapes=[pltpu.VMEM((deep, rows, wide), train.dtype), pltpu.SemaphoreType.DMA((deep,))],
        compiler_params=pltpu.CompilerParams(vmem_limit_bytes=16 << 20),
        cost_estimate=pl.CostEstimate(flops=2 << 30, bytes_accessed=8 << 20, transcendentals=0),
        name="transpose_%d" % layer,
    )(pltpu.with_memory_space_constraint(train, pltpu.HBM))


def layer_score(turned, rows):
    rows = [row[...] for row in rows]
    count = sum(row.shape[0] for row in rows)
    rows = rows * max(1, 128 // count)
    return dot(jnp.concatenate(rows, axis=0), turned[...])[:count]


def pieces(unit, layer):
    if not isinstance(unit, (list, tuple)):
        return [unit.at[layer]]
    half = len(unit) // 2
    return [piece.at[0] for piece in unit[layer * half:(layer + 1) * half]]


def score(turned, more, units):
    return sum(
        layer_score(t, [piece for unit in units for piece in pieces(unit, layer)])
        for layer, t in enumerate((turned, more))
    )


def chip_at(offset):
    row = lax.axis_index("row")
    chip, core = row // 2, lax.rem(row, 2)
    up, column = chip // 2, lax.rem(chip, 2)
    place = jnp.where(column == 0, up, 7 - up) - offset * (1 - 2 * core)
    place = lax.rem(place + 8, 8)
    return jnp.where(place < 4, 2 * place, 2 * (7 - place) + 1)


def foreign(offset):
    return chip_at(offset) // 4 != lax.axis_index("layer")


def put(out, at, offset, block):
    rows = block.shape[0] // 2
    core = lax.rem(lax.axis_index("row"), 2)
    if offset < 0:
        core = 1 - core
    start = (at - 4 * lax.axis_index("layer")) * 2 * rows
    out[pl.ds(pl.multiple_of(start + core * rows, rows), rows), :] = block[:rows]
    out[pl.ds(pl.multiple_of(start + (1 - core) * rows, rows), rows), :] = block[rows:]


def split(offset, ahead, behind, sent, kept):
    @pl.when(foreign(offset))
    def _():
        sent[...] = ahead[...].astype(sent.dtype)
        kept[...] = behind[...]

    @pl.when(jnp.logical_not(foreign(offset)))
    def _():
        sent[...] = behind[...].astype(sent.dtype)
        kept[...] = ahead[...]


def plain_kernel(turned, more, *refs):
    refs[-1][...] = score(turned, more, refs[:-1])


def second_kernel(turned, more, own, *refs):
    *queries, sent, kept, total = refs
    half = kept.shape[0]
    total[...] = score(turned, more, [*queries[:3], queries[3:]])
    split(2, total.at[:half], total.at[half:], sent.at[:half], kept)
    sent[half:] = own[...].astype(sent.dtype)


def third_kernel(turned, more, first, *refs):
    *queries, sent, kept, total = refs
    half = total.shape[0] // 2
    total[...] = score(turned, more, [*queries[:3], queries[3:]])
    split(1, first.at[:half], total.at[half:], sent.at[:half], kept.at[:half])
    split(3, total.at[:half], first.at[half:], sent.at[half:2 * half], kept.at[half:])


def opening_kernel(turned, *refs):
    unit, *swapped, out = refs
    out[...] = layer_score(turned, [unit.at[0]] + [ref.at[0] for ref in swapped])


def second_layer(turned, opening, unit, swapped):
    return opening[...] + layer_score(turned, [unit.at[1]] + [ref.at[0] for ref in swapped])


def fourth_kernel(turned, opening, *refs):
    unit, *swapped, sent = refs

    @pl.when(foreign(4))
    def _():
        sent[...] = second_layer(turned, opening, unit, swapped).astype(sent.dtype)

    @pl.when(jnp.logical_not(foreign(4)))
    def _():
        sent[...] = jnp.zeros_like(sent)


def fifth_kernel(turned, opening, *refs):
    unit, *swapped, kept = refs

    @pl.when(jnp.logical_not(foreign(4)))
    def _():
        kept[...] = second_layer(turned, opening, unit, swapped)


def block_call(kernel, name, rows, total, turned, operands, kind=jnp.float32, sent=0):
    columns = turned[0].shape[1]
    block = jax.ShapeDtypeStruct((rows, columns), jnp.float32)
    one = total is None
    return pl.pallas_call(
        kernel,
        out_shape=(jax.ShapeDtypeStruct((max(rows, sent), columns), kind), block) if not one else jax.ShapeDtypeStruct(block.shape, kind),
        in_specs=[VMEM] * (len(turned) + len(operands)),
        out_specs=VMEM if one else (VMEM, VMEM),
        scratch_shapes=[pltpu.VMEM((total, columns), jnp.float32)] if total else [],
        compiler_params=pltpu.CompilerParams(vmem_limit_bytes=24 << 20),
        cost_estimate=pl.CostEstimate(flops=1 << 10, bytes_accessed=1 << 10, transcendentals=0),
        name=name,
    )(*turned, *operands)


def gather_kernel(kept2, got2, kept13, got13, own, out):
    rows = kept2.shape[0]
    low, high = pl.ds(0, rows), pl.ds(rows, rows)
    for offset, kept, got in (
        (2, kept2, got2.at[low]),
        (1, kept13.at[low], got13.at[low]),
        (3, kept13.at[high], got13.at[high]),
    ):
        block = kept[...] + got[...].astype(kept.dtype)

        @pl.when(foreign(offset))
        def _():
            put(out, chip_at(offset - 4), offset - 4, block)

        @pl.when(jnp.logical_not(foreign(offset)))
        def _():
            put(out, chip_at(offset), offset, block)

    @pl.when(foreign(4))
    def _():
        put(out, chip_at(0), 0, own[...] + got2[high].astype(own.dtype))


def last_kernel(kept, got, table, out, block, sems):
    del table

    @pl.when(jnp.logical_not(foreign(4)))
    def _():
        rows = kept.shape[0] // 2
        block[...] = kept[...] + got[...].astype(kept.dtype)
        at = chip_at(4) - 4 * lax.axis_index("layer")
        core = lax.rem(lax.axis_index("row"), 2)
        copies = []
        for n, c in enumerate((core, 1 - core)):
            start = pl.multiple_of((2 * at + c) * rows, rows)
            copies.append(
                pltpu.make_async_copy(block.at[n * rows:(n + 1) * rows], out.at[pl.ds(start, rows)], sems.at[n])
            )
        for copy in copies:
            copy.start()
        for copy in copies:
            copy.wait()


def finish(most, last, rows, columns):
    table = jax.ShapeDtypeStruct((rows, columns), jnp.float32)
    params = pltpu.CompilerParams(vmem_limit_bytes=8 << 20)
    gathered = pl.pallas_call(
        gather_kernel,
        out_shape=table,
        in_specs=[VMEM] * 5,
        out_specs=VMEM,
        compiler_params=params,
        cost_estimate=pl.CostEstimate(flops=60 << 30, bytes_accessed=1 << 20, transcendentals=0),
        name="gather_rows",
    )(*most)
    return pl.pallas_call(
        last_kernel,
        out_shape=table,
        in_specs=[VMEM, VMEM, HBM],
        out_specs=HBM,
        scratch_shapes=[pltpu.VMEM(last[0].shape, jnp.float32), pltpu.SemaphoreType.DMA((2,))],
        input_output_aliases={2: 0},
        compiler_params=params,
        name="last_rows",
    )(*last, gathered)


def ring_order(chips):
    wide = chips // 4
    order = [(i, 0) for i in range(4)]
    for turn, i in enumerate(reversed(range(4))):
        others = range(1, wide)
        order += [(i, j) for j in (reversed(others) if turn % 2 else others)]
    return [i * wide + j for i, j in order]


def ring_pairs(groups, chips, cores=2):
    order = ring_order(chips)
    flat = lambda layer, chip, core: (layer * chips + chip) * cores + core
    every = [(y, h, c) for y in range(groups) for h in range(chips) for c in range(cores)]
    step = lambda h, c: order[(order.index(h) + (1 - 2 * c)) % chips]
    swap = [(flat(y, h, c), flat(y, h, 1 - c)) for y, h, c in every]
    around = [(flat(y, h, c), flat(y, step(h, c), c)) for y, h, c in every]
    across = [(flat(y, h, c), flat(groups - 1 - y, h, c)) for y, h, c in every]
    return swap, around, across


def send(value, pairs):
    return lax.ppermute(value, AXES, pairs)


def any_ring_device(groups, chips, query_grads, train_grads, left_inverse, right_inverse):
    swap, around, _ = ring_pairs(groups, chips)
    order = ring_order(chips)
    mine = precondition(query_grads, left_inverse, right_inverse, True)
    turned = [transpose(l, train_grads) for l in range(query_grads.shape[0])]
    rows = mine.shape[1]
    row = lax.axis_index("row")
    chip, core = row // 2, lax.rem(row, 2)
    place = jnp.argmax(jnp.array(order, jnp.int32) == chip).astype(jnp.int32)
    table = jnp.zeros((chips * 2 * rows, train_grads.shape[1]), jnp.float32)

    def fill(table, block, offset, core):
        at = lax.rem(place + offset * (1 - 2 * lax.rem(row, 2)) + chips, chips)
        at = lax.dynamic_index_in_dim(jnp.array(order, jnp.int32), at, 0, keepdims=False) * 2 + core
        return lax.dynamic_update_slice_in_dim(table, block, at * rows, 0)

    held = [mine, send(mine, swap)]
    block = block_call(plain_kernel, "scores", 2 * rows, None, turned, held)
    table = fill(table, block[:rows], 0, core)
    table = fill(table, block[rows:], 0, 1 - core)
    for k in range(1, chips // 2 + 1):
        held = [send(h, around) for h in (held if k < chips // 2 else held[:1])]
        queries = held + [send(h, swap) for h in held]
        block = block_call(plain_kernel, "scores", len(queries) * rows, None, turned, queries)
        cores = (core, 1 - core, 1 - core, core) if len(held) == 2 else (core, 1 - core)
        for n, c in enumerate(cores):
            table = fill(table, block[n * rows:(n + 1) * rows], -k if n < len(held) or k == chips // 2 else k, c)
    return lax.psum_scatter(table, "layer", scatter_dimension=0, tiled=True)


def ring_device(query_grads, train_grads, left_inverse, right_inverse):
    chips, groups = 8, 2
    swap, around, across = ring_pairs(groups, chips)
    after = lax.optimization_barrier

    def quarters(unit):
        layers, held, feat = unit.shape
        half = held // 2
        return [send(unit[l:l + 1, n:n + half], swap) for l in range(layers) for n in (0, half)]

    halves_of = lambda unit: [send(unit[l:l + 1], swap) for l in range(unit.shape[0])]

    arrived = [send(query_grads, around), send(send(query_grads, swap), around)]
    mine = precondition(query_grads, left_inverse, right_inverse, True)
    a, b = [mine], [send(mine, swap)]
    turned = [transpose(l, train_grads) for l in range(2)]
    arrived[0], *turned = after((arrived[0], *turned))
    a.append(precondition(arrived[0], left_inverse, right_inverse, False))
    b.append(precondition(arrived[1], left_inverse, right_inverse, False))
    rows = 2 * mine.shape[1]
    zeroth = block_call(plain_kernel, "scores_0", rows, None, turned, [a[0], b[0]])
    a.append(send(a[1], around))
    b.append(send(b[1], around))
    first = block_call(plain_kernel, "scores_1", 2 * rows, None, turned, [a[1], b[1], send(a[1], swap), send(b[1], swap)])
    a.append(send(a[2], around))
    b[2], first, _ = after((b[2], first, mine))
    b.append(send(b[2], around))
    queries = [a[2], b[2], send(a[2], swap), *halves_of(b[2])]
    sent2, kept2 = block_call(second_kernel, "scores_2", rows, 2 * rows, turned, [zeroth] + queries, jnp.bfloat16, 2 * rows)
    a[3], _ = after((a[3], sent2))
    a.append(send(a[3], around))
    got2 = send(sent2, across)
    b[3], got2 = after((b[3], got2))
    queries = [a[3], b[3], send(a[3], swap), *halves_of(b[3])]
    sent, kept = block_call(third_kernel, "scores_3", 2 * rows, 2 * rows, turned, [first] + queries, jnp.bfloat16, 2 * rows + 32)
    got = send(sent, across)
    a[4], _ = after((a[4], sent))
    swapped = quarters(a[4])
    opening = block_call(opening_kernel, "scores_4", rows, None, turned[:1], [a[4], *swapped[:2]])
    sent4 = block_call(fourth_kernel, "scores_5", rows, None, turned[1:], [opening, a[4], *swapped[2:]], jnp.bfloat16)
    got4 = send(sent4, across)
    kept4 = block_call(fifth_kernel, "scores_6", rows, None, turned[1:], [opening, a[4], *swapped[2:]])
    return finish((kept2, got2, kept, got, zeroth), (kept4, got4), chips // groups * rows, turned[0].shape[1])


def solution(mesh):
    placed = (
        P("layer", "row", None),
        P("layer", "row", None),
        P("layer", None, None),
        P("layer", None, None),
    )
    groups, chips = mesh.shape["layer"], mesh.shape["row"] // 2
    if (groups, chips) == (2, 8):
        on_device = ring_device
    else:
        on_device = functools.partial(any_ring_device, groups, chips)
    return jax.shard_map(
        on_device, mesh=mesh, in_specs=placed, out_specs=P("layer", "row"), check_vma=False
    )
```

```python
import functools

import jax
import jax.numpy as jnp
from jax import lax
from jax.experimental import pallas as pl
from jax.experimental.pallas import tpu as pltpu
from jax.sharding import PartitionSpec as P

AXES = ("layer", "row")
VMEM = pl.BlockSpec(memory_space=pltpu.VMEM)
HBM = pl.BlockSpec(memory_space=pl.ANY)


def halves(v):
    top = v.astype(jnp.bfloat16)
    return top, (v - top.astype(jnp.float32)).astype(jnp.bfloat16)


def dot(a, b):
    return jnp.dot(a, b, preferred_element_type=jnp.float32)


def precondition_first_kernel(query_hbm, left_hbm, right_hbm, out, query, left, right, *refs):
    *scratch, sems = refs
    copies = [
        pltpu.make_async_copy(src, dst, sems.at[n])
        for n, (src, dst) in enumerate(((left_hbm, left), (right_hbm, right), (query_hbm, query)))
    ]
    for copy in copies:
        copy.start()
    copies[0].wait()
    copies[1].wait()
    precondition_kernel(query, left, right, out, *scratch, arrived=copies[2].wait)


def precondition_kernel(query, left, right, out, turned, mixed, arrived=lambda: None):
    layers, rows, feat = query.shape
    proj = left.shape[1]
    half, pairs, stride = proj // 2, feat // 128, mixed.shape[1] // (feat // 128)
    i = lax.broadcasted_iota(jnp.int32, (2 * proj, 4 * proj), 0) // proj
    j = lax.broadcasted_iota(jnp.int32, (2 * proj, 4 * proj), 1) // (2 * proj)
    same = i == j
    i = lax.broadcasted_iota(jnp.int32, (proj, proj), 0)
    j = lax.broadcasted_iota(jnp.int32, (proj, proj), 1)
    pick = (j == 2 * lax.rem(i, half) + i // half).astype(jnp.bfloat16)
    pick_t = (i == 2 * lax.rem(j, half) + j // half).astype(jnp.bfloat16)
    rights, lefts = [], []
    for l in range(layers):
        wide = jnp.concatenate([right[l], right[l]], axis=1)
        wide = jnp.concatenate([wide, wide], axis=1)
        wide = jnp.where(same, jnp.concatenate([wide, wide], axis=0), 0.0)
        rights.append(jnp.concatenate(halves(wide), axis=0))
        high, low = halves(left[l])
        both = dot(pick, jnp.concatenate([high, low], axis=1)).astype(jnp.bfloat16)
        high, low = (dot(both[:, n:n + proj], pick_t).astype(jnp.bfloat16) for n in (0, proj))
        lefts.append(jnp.concatenate([high, low, high], axis=1))
    arrived()
    for l in range(layers):
        x = jnp.concatenate([query[l, :, k * 128:(k + 1) * 128] for k in range(pairs)], axis=0)
        y = dot(jnp.concatenate([x, x], axis=1), rights[l])
        for p in range(2):
            for k in range(pairs):
                turned[l, p, k * stride:k * stride + rows] = y[k * rows:(k + 1) * rows, p * 128:(p + 1) * 128]
    step = 8
    first = lax.rem(lax.broadcasted_iota(jnp.int32, (pairs, step * 128), 1), 128) < proj
    for l in range(layers):
        for q in range(0, rows, step):
            y = [
                jnp.concatenate([turned[l, p, pl.ds(q + n, pairs, stride=stride), :] for n in range(step)], axis=1)
                for p in range(2)
            ]
            high, low = halves(jnp.concatenate(y, axis=0))
            z = dot(lefts[l], jnp.concatenate([high, high, low], axis=0))
            z = jnp.where(first, z[:half], z[half:])
            for n in range(step):
                mixed[l, pl.ds(q + n, pairs, stride=stride), :] = z[:, n * 128:(n + 1) * 128]
        for m in range(pairs):
            out[l, :, m * 128:(m + 1) * 128] = mixed[l, m * stride:m * stride + rows].astype(jnp.bfloat16)


def precondition(query, left, right, first):
    layers, rows, feat = query.shape
    spread = (rows + 8) * feat // 128
    scratch = [pltpu.VMEM((layers, 2, spread, 128), jnp.float32), pltpu.VMEM((layers, spread, 128), jnp.float32)]
    operands = (query, left, right)
    if first:
        scratch = [pltpu.VMEM(v.shape, v.dtype) for v in operands] + scratch + [pltpu.SemaphoreType.DMA((3,))]
        operands = [pltpu.with_memory_space_constraint(v, pltpu.HBM) for v in operands]
    return pl.pallas_call(
        precondition_first_kernel if first else precondition_kernel,
        out_shape=jax.ShapeDtypeStruct(query.shape, jnp.bfloat16),
        in_specs=[HBM if first else VMEM] * 3,
        out_specs=VMEM,
        scratch_shapes=scratch,
        compiler_params=pltpu.CompilerParams(vmem_limit_bytes=16 << 20),
        cost_estimate=pl.CostEstimate(flops=2 << 30, bytes_accessed=4 << 20, transcendentals=0),
        name="precondition_0" if first else "precondition_1",
    )(*operands)


def transpose_kernel(layer, train, out, buffer, sems):
    feat = train.shape[2]
    deep, rows, wide = buffer.shape
    steps = feat // wide

    def copy(n):
        return pltpu.make_async_copy(train.at[layer, :, pl.ds(n * wide, wide)], buffer.at[n % deep], sems.at[n % deep])

    for n in range(deep):
        copy(n).start()
    for n in range(steps):
        copy(n).wait()
        out[n * wide:(n + 1) * wide, :] = buffer[n % deep].T
        if n + deep < steps:
            copy(n + deep).start()


def transpose(layer, train):
    layers, rows, feat = train.shape
    wide, deep = 512, 8
    return pl.pallas_call(
        functools.partial(transpose_kernel, layer),
        out_shape=pltpu.VMEM((feat, rows), train.dtype),
        in_specs=[HBM],
        out_specs=VMEM,
        scratch_shapes=[pltpu.VMEM((deep, rows, wide), train.dtype), pltpu.SemaphoreType.DMA((deep,))],
        compiler_params=pltpu.CompilerParams(vmem_limit_bytes=16 << 20),
        cost_estimate=pl.CostEstimate(flops=2 << 30, bytes_accessed=8 << 20, transcendentals=0),
        name="transpose_%d" % layer,
    )(pltpu.with_memory_space_constraint(train, pltpu.HBM))


def layer_score(turned, rows):
    rows = [row[...] for row in rows]
    count = sum(row.shape[0] for row in rows)
    rows = rows * max(1, 128 // count)
    return dot(jnp.concatenate(rows, axis=0), turned[...])[:count]


def pieces(unit, layer):
    if not isinstance(unit, (list, tuple)):
        return [unit.at[layer]]
    half = len(unit) // 2
    return [piece.at[0] for piece in unit[layer * half:(layer + 1) * half]]


def score(turned, more, units):
    return sum(
        layer_score(t, [piece for unit in units for piece in pieces(unit, layer)])
        for layer, t in enumerate((turned, more))
    )


def chip_at(offset):
    row = lax.axis_index("row")
    chip, core = row // 2, lax.rem(row, 2)
    up, column = chip // 2, lax.rem(chip, 2)
    place = jnp.where(column == 0, up, 7 - up) - offset * (1 - 2 * core)
    place = lax.rem(place + 8, 8)
    return jnp.where(place < 4, 2 * place, 2 * (7 - place) + 1)


def foreign(offset):
    return chip_at(offset) // 4 != lax.axis_index("layer")


def put(out, at, offset, block):
    rows = block.shape[0] // 2
    core = lax.rem(lax.axis_index("row"), 2)
    if offset < 0:
        core = 1 - core
    start = (at - 4 * lax.axis_index("layer")) * 2 * rows
    out[pl.ds(pl.multiple_of(start + core * rows, rows), rows), :] = block[:rows]
    out[pl.ds(pl.multiple_of(start + (1 - core) * rows, rows), rows), :] = block[rows:]


def split(offset, ahead, behind, sent, kept):
    @pl.when(foreign(offset))
    def _():
        sent[...] = ahead[...].astype(sent.dtype)
        kept[...] = behind[...]

    @pl.when(jnp.logical_not(foreign(offset)))
    def _():
        sent[...] = behind[...].astype(sent.dtype)
        kept[...] = ahead[...]


def plain_kernel(turned, more, *refs):
    refs[-1][...] = score(turned, more, refs[:-1])


def second_kernel(turned, more, own, *refs):
    *queries, sent, kept, total = refs
    half = kept.shape[0]
    total[...] = score(turned, more, [*queries[:3], queries[3:]])
    split(2, total.at[:half], total.at[half:], sent.at[:half], kept)
    sent[half:] = own[...].astype(sent.dtype)


def third_kernel(turned, more, first, *refs):
    *queries, sent, kept, total = refs
    half = total.shape[0] // 2
    total[...] = score(turned, more, [*queries[:3], queries[3:]])
    split(1, first.at[:half], total.at[half:], sent.at[:half], kept.at[:half])
    split(3, total.at[:half], first.at[half:], sent.at[half:2 * half], kept.at[half:])


def opening_kernel(turned, *refs):
    unit, *swapped, out = refs
    out[...] = layer_score(turned, [unit.at[0]] + [ref.at[0] for ref in swapped])


def second_layer(turned, opening, unit, swapped):
    return opening[...] + layer_score(turned, [unit.at[1]] + [ref.at[0] for ref in swapped])


def fourth_kernel(turned, opening, *refs):
    unit, *swapped, sent = refs

    @pl.when(foreign(4))
    def _():
        sent[...] = second_layer(turned, opening, unit, swapped).astype(sent.dtype)

    @pl.when(jnp.logical_not(foreign(4)))
    def _():
        sent[...] = jnp.zeros_like(sent)


def fifth_kernel(turned, opening, *refs):
    unit, *swapped, kept = refs

    @pl.when(jnp.logical_not(foreign(4)))
    def _():
        kept[...] = second_layer(turned, opening, unit, swapped)


def block_call(kernel, name, rows, total, turned, operands, kind=jnp.float32, sent=0):
    columns = turned[0].shape[1]
    block = jax.ShapeDtypeStruct((rows, columns), jnp.float32)
    one = total is None
    return pl.pallas_call(
        kernel,
        out_shape=(jax.ShapeDtypeStruct((max(rows, sent), columns), kind), block) if not one else jax.ShapeDtypeStruct(block.shape, kind),
        in_specs=[VMEM] * (len(turned) + len(operands)),
        out_specs=VMEM if one else (VMEM, VMEM),
        scratch_shapes=[pltpu.VMEM((total, columns), jnp.float32)] if total else [],
        compiler_params=pltpu.CompilerParams(vmem_limit_bytes=24 << 20),
        cost_estimate=pl.CostEstimate(flops=1 << 10, bytes_accessed=1 << 10, transcendentals=0),
        name=name,
    )(*turned, *operands)


def gather_kernel(kept2, got2, kept13, got13, own, out):
    rows = kept2.shape[0]
    low, high = pl.ds(0, rows), pl.ds(rows, rows)
    for offset, kept, got in (
        (2, kept2, got2.at[low]),
        (1, kept13.at[low], got13.at[low]),
        (3, kept13.at[high], got13.at[high]),
    ):
        block = kept[...] + got[...].astype(kept.dtype)

        @pl.when(foreign(offset))
        def _():
            put(out, chip_at(offset - 4), offset - 4, block)

        @pl.when(jnp.logical_not(foreign(offset)))
        def _():
            put(out, chip_at(offset), offset, block)

    @pl.when(foreign(4))
    def _():
        put(out, chip_at(0), 0, own[...] + got2[high].astype(own.dtype))


def last_kernel(kept, got, table, out, block, sem):
    del table

    @pl.when(jnp.logical_not(foreign(4)))
    def _():
        rows = kept.shape[0] // 2
        core = lax.rem(lax.axis_index("row"), 2)
        for n, c in enumerate((core, 1 - core)):
            part = pl.ds(n * rows, rows)
            block[pl.ds(pl.multiple_of(c * rows, rows), rows), :] = kept[part, :] + got[part, :].astype(kept.dtype)
        start = pl.multiple_of((chip_at(4) - 4 * lax.axis_index("layer")) * 2 * rows, 2 * rows)
        copy = pltpu.make_async_copy(block, out.at[pl.ds(start, 2 * rows)], sem)
        copy.start()
        copy.wait()


def finish(most, last, rows, columns):
    table = jax.ShapeDtypeStruct((rows, columns), jnp.float32)
    params = pltpu.CompilerParams(vmem_limit_bytes=8 << 20)
    gathered = pl.pallas_call(
        gather_kernel,
        out_shape=table,
        in_specs=[VMEM] * 5,
        out_specs=VMEM,
        compiler_params=params,
        cost_estimate=pl.CostEstimate(flops=1 << 30, bytes_accessed=1 << 20, transcendentals=0),
        name="gather_rows",
    )(*most)
    return pl.pallas_call(
        last_kernel,
        out_shape=table,
        in_specs=[VMEM, VMEM, HBM],
        out_specs=HBM,
        scratch_shapes=[pltpu.VMEM(last[0].shape, jnp.float32), pltpu.SemaphoreType.DMA],
        input_output_aliases={2: 0},
        compiler_params=params,
        name="last_rows",
    )(*last, gathered)


def ring_order(chips):
    wide = chips // 4
    order = [(i, 0) for i in range(4)]
    for turn, i in enumerate(reversed(range(4))):
        others = range(1, wide)
        order += [(i, j) for j in (reversed(others) if turn % 2 else others)]
    return [i * wide + j for i, j in order]


def ring_pairs(groups, chips, cores=2):
    order = ring_order(chips)
    flat = lambda layer, chip, core: (layer * chips + chip) * cores + core
    every = [(y, h, c) for y in range(groups) for h in range(chips) for c in range(cores)]
    step = lambda h, c: order[(order.index(h) + (1 - 2 * c)) % chips]
    swap = [(flat(y, h, c), flat(y, h, 1 - c)) for y, h, c in every]
    around = [(flat(y, h, c), flat(y, step(h, c), c)) for y, h, c in every]
    across = [(flat(y, h, c), flat(groups - 1 - y, h, c)) for y, h, c in every]
    return swap, around, across


def send(value, pairs):
    return lax.ppermute(value, AXES, pairs)


def any_ring_device(groups, chips, query_grads, train_grads, left_inverse, right_inverse):
    swap, around, _ = ring_pairs(groups, chips)
    order = ring_order(chips)
    mine = precondition(query_grads, left_inverse, right_inverse, True)
    turned = [transpose(l, train_grads) for l in range(query_grads.shape[0])]
    rows = mine.shape[1]
    row = lax.axis_index("row")
    chip, core = row // 2, lax.rem(row, 2)
    place = jnp.argmax(jnp.array(order, jnp.int32) == chip).astype(jnp.int32)
    table = jnp.zeros((chips * 2 * rows, train_grads.shape[1]), jnp.float32)

    def fill(table, block, offset, core):
        at = lax.rem(place + offset * (1 - 2 * lax.rem(row, 2)) + chips, chips)
        at = lax.dynamic_index_in_dim(jnp.array(order, jnp.int32), at, 0, keepdims=False) * 2 + core
        return lax.dynamic_update_slice_in_dim(table, block, at * rows, 0)

    held = [mine, send(mine, swap)]
    block = block_call(plain_kernel, "scores", 2 * rows, None, turned, held)
    table = fill(table, block[:rows], 0, core)
    table = fill(table, block[rows:], 0, 1 - core)
    for k in range(1, chips // 2 + 1):
        held = [send(h, around) for h in (held if k < chips // 2 else held[:1])]
        queries = held + [send(h, swap) for h in held]
        block = block_call(plain_kernel, "scores", len(queries) * rows, None, turned, queries)
        cores = (core, 1 - core, 1 - core, core) if len(held) == 2 else (core, 1 - core)
        for n, c in enumerate(cores):
            table = fill(table, block[n * rows:(n + 1) * rows], -k if n < len(held) or k == chips // 2 else k, c)
    return lax.psum_scatter(table, "layer", scatter_dimension=0, tiled=True)


def ring_device(query_grads, train_grads, left_inverse, right_inverse):
    chips, groups = 8, 2
    swap, around, across = ring_pairs(groups, chips)
    after = lax.optimization_barrier

    def quarters(unit):
        layers, held, feat = unit.shape
        half = held // 2
        return [send(unit[l:l + 1, n:n + half], swap) for l in range(layers) for n in (0, half)]

    halves_of = lambda unit: [send(unit[l:l + 1], swap) for l in range(unit.shape[0])]

    arrived = [send(query_grads, around), send(send(query_grads, swap), around)]
    mine = precondition(query_grads, left_inverse, right_inverse, True)
    a, b = [mine], [send(mine, swap)]
    turned = [transpose(l, train_grads) for l in range(2)]
    arrived[0], *turned = after((arrived[0], *turned))
    a.append(precondition(arrived[0], left_inverse, right_inverse, False))
    b.append(precondition(arrived[1], left_inverse, right_inverse, False))
    rows = 2 * mine.shape[1]
    zeroth = block_call(plain_kernel, "scores_0", rows, None, turned, [a[0], b[0]])
    a.append(send(a[1], around))
    b.append(send(b[1], around))
    first = block_call(plain_kernel, "scores_1", 2 * rows, None, turned, [a[1], b[1], send(a[1], swap), send(b[1], swap)])
    a.append(send(a[2], around))
    b[2], first, _ = after((b[2], first, mine))
    b.append(send(b[2], around))
    queries = [a[2], b[2], send(a[2], swap), *halves_of(b[2])]
    sent2, kept2 = block_call(second_kernel, "scores_2", rows, 2 * rows, turned, [zeroth] + queries, jnp.bfloat16, 2 * rows)
    a[3], _ = after((a[3], sent2))
    a.append(send(a[3], around))
    got2 = send(sent2, across)
    b[3], got2 = after((b[3], got2))
    queries = [a[3], b[3], send(a[3], swap), *halves_of(b[3])]
    sent, kept = block_call(third_kernel, "scores_3", 2 * rows, 2 * rows, turned, [first] + queries, jnp.bfloat16, 2 * rows + 16)
    got = send(sent, across)
    a[4], _ = after((a[4], sent))
    swapped = quarters(a[4])
    opening = block_call(opening_kernel, "scores_4", rows, None, turned[:1], [a[4], *swapped[:2]])
    sent4 = block_call(fourth_kernel, "scores_5", rows, None, turned[1:], [opening, a[4], *swapped[2:]], jnp.bfloat16)
    got4 = send(sent4, across)
    kept4 = block_call(fifth_kernel, "scores_6", rows, None, turned[1:], [opening, a[4], *swapped[2:]])
    return finish((kept2, got2, kept, got, zeroth), (kept4, got4), chips // groups * rows, turned[0].shape[1])


def solution(mesh):
    placed = (
        P("layer", "row", None),
        P("layer", "row", None),
        P("layer", None, None),
        P("layer", None, None),
    )
    groups, chips = mesh.shape["layer"], mesh.shape["row"] // 2
    if (groups, chips) == (2, 8):
        on_device = ring_device
    else:
        on_device = functools.partial(any_ring_device, groups, chips)
    return jax.shard_map(
        on_device, mesh=mesh, in_specs=placed, out_specs=P("layer", "row"), check_vma=False
    )
```

```python
import functools

import jax
import jax.numpy as jnp
from jax import lax
from jax.experimental import pallas as pl
from jax.experimental.pallas import tpu as pltpu
from jax.sharding import PartitionSpec as P

AXES = ("layer", "row")
VMEM = pl.BlockSpec(memory_space=pltpu.VMEM)
HBM = pl.BlockSpec(memory_space=pl.ANY)


def halves(v):
    top = v.astype(jnp.bfloat16)
    return top, (v - top.astype(jnp.float32)).astype(jnp.bfloat16)


def dot(a, b):
    return jnp.dot(a, b, preferred_element_type=jnp.float32)


def precondition_first_kernel(query_hbm, left_hbm, right_hbm, out, query, left, right, *refs):
    *scratch, sems = refs
    copies = [
        pltpu.make_async_copy(src, dst, sems.at[n])
        for n, (src, dst) in enumerate(((left_hbm, left), (right_hbm, right), (query_hbm, query)))
    ]
    for copy in copies:
        copy.start()
    copies[0].wait()
    copies[1].wait()
    precondition_kernel(query, left, right, out, *scratch, arrived=copies[2].wait)


def precondition_kernel(query, left, right, out, turned, mixed, arrived=lambda: None):
    layers, rows, feat = query.shape
    proj = left.shape[1]
    half, pairs, stride = proj // 2, feat // 128, mixed.shape[1] // (feat // 128)
    i = lax.broadcasted_iota(jnp.int32, (2 * proj, 4 * proj), 0) // proj
    j = lax.broadcasted_iota(jnp.int32, (2 * proj, 4 * proj), 1) // (2 * proj)
    same = i == j
    i = lax.broadcasted_iota(jnp.int32, (proj, proj), 0)
    j = lax.broadcasted_iota(jnp.int32, (proj, proj), 1)
    pick = (j == 2 * lax.rem(i, half) + i // half).astype(jnp.bfloat16)
    pick_t = (i == 2 * lax.rem(j, half) + j // half).astype(jnp.bfloat16)
    rights, lefts = [], []
    for l in range(layers):
        wide = jnp.concatenate([right[l], right[l]], axis=1)
        wide = jnp.concatenate([wide, wide], axis=1)
        wide = jnp.where(same, jnp.concatenate([wide, wide], axis=0), 0.0)
        rights.append(jnp.concatenate(halves(wide), axis=0))
        high, low = halves(left[l])
        both = dot(pick, jnp.concatenate([high, low], axis=1)).astype(jnp.bfloat16)
        high, low = (dot(both[:, n:n + proj], pick_t).astype(jnp.bfloat16) for n in (0, proj))
        lefts.append(jnp.concatenate([high, low, high], axis=1))
    arrived()
    for l in range(layers):
        x = jnp.concatenate([query[l, :, k * 128:(k + 1) * 128] for k in range(pairs)], axis=0)
        y = dot(jnp.concatenate([x, x], axis=1), rights[l])
        for p in range(2):
            for k in range(pairs):
                turned[l, p, k * stride:k * stride + rows] = y[k * rows:(k + 1) * rows, p * 128:(p + 1) * 128]
    step = 8
    first = lax.rem(lax.broadcasted_iota(jnp.int32, (pairs, step * 128), 1), 128) < proj
    for l in range(layers):
        for q in range(0, rows, step):
            y = [
                jnp.concatenate([turned[l, p, pl.ds(q + n, pairs, stride=stride), :] for n in range(step)], axis=1)
                for p in range(2)
            ]
            high, low = halves(jnp.concatenate(y, axis=0))
            z = dot(lefts[l], jnp.concatenate([high, high, low], axis=0))
            z = jnp.where(first, z[:half], z[half:])
            for n in range(step):
                mixed[l, pl.ds(q + n, pairs, stride=stride), :] = z[:, n * 128:(n + 1) * 128]
        for m in range(pairs):
            out[l, :, m * 128:(m + 1) * 128] = mixed[l, m * stride:m * stride + rows].astype(jnp.bfloat16)


def precondition(query, left, right, first):
    layers, rows, feat = query.shape
    spread = (rows + 8) * feat // 128
    scratch = [pltpu.VMEM((layers, 2, spread, 128), jnp.float32), pltpu.VMEM((layers, spread, 128), jnp.float32)]
    operands = (query, left, right)
    if first:
        scratch = [pltpu.VMEM(v.shape, v.dtype) for v in operands] + scratch + [pltpu.SemaphoreType.DMA((3,))]
        operands = [pltpu.with_memory_space_constraint(v, pltpu.HBM) for v in operands]
    return pl.pallas_call(
        precondition_first_kernel if first else precondition_kernel,
        out_shape=jax.ShapeDtypeStruct(query.shape, jnp.bfloat16),
        in_specs=[HBM if first else VMEM] * 3,
        out_specs=VMEM,
        scratch_shapes=scratch,
        compiler_params=pltpu.CompilerParams(vmem_limit_bytes=16 << 20),
        cost_estimate=pl.CostEstimate(flops=2 << 30, bytes_accessed=4 << 20, transcendentals=0),
        name="precondition_0" if first else "precondition_1",
    )(*operands)


def transpose_kernel(layer, train, out, buffer, sems):
    feat = train.shape[2]
    deep, rows, wide = buffer.shape
    steps = feat // wide

    def copy(n):
        return pltpu.make_async_copy(train.at[layer, :, pl.ds(n * wide, wide)], buffer.at[n % deep], sems.at[n % deep])

    for n in range(deep):
        copy(n).start()
    for n in range(steps):
        copy(n).wait()
        out[n * wide:(n + 1) * wide, :] = buffer[n % deep].T
        if n + deep < steps:
            copy(n + deep).start()


def transpose(layer, train):
    layers, rows, feat = train.shape
    wide, deep = 512, 8
    return pl.pallas_call(
        functools.partial(transpose_kernel, layer),
        out_shape=pltpu.VMEM((feat, rows), train.dtype),
        in_specs=[HBM],
        out_specs=VMEM,
        scratch_shapes=[pltpu.VMEM((deep, rows, wide), train.dtype), pltpu.SemaphoreType.DMA((deep,))],
        compiler_params=pltpu.CompilerParams(vmem_limit_bytes=16 << 20),
        cost_estimate=pl.CostEstimate(flops=2 << 30, bytes_accessed=8 << 20, transcendentals=0),
        name="transpose_%d" % layer,
    )(pltpu.with_memory_space_constraint(train, pltpu.HBM))


def layer_score(turned, rows):
    rows = [row[...] for row in rows]
    count = sum(row.shape[0] for row in rows)
    rows = rows * max(1, 128 // count)
    return dot(jnp.concatenate(rows, axis=0), turned[...])[:count]


def pieces(unit, layer):
    if not isinstance(unit, (list, tuple)):
        return [unit.at[layer]]
    half = len(unit) // 2
    return [piece.at[0] for piece in unit[layer * half:(layer + 1) * half]]


def score(turned, more, units):
    return sum(
        layer_score(t, [piece for unit in units for piece in pieces(unit, layer)])
        for layer, t in enumerate((turned, more))
    )


def chip_at(offset):
    row = lax.axis_index("row")
    chip, core = row // 2, lax.rem(row, 2)
    up, column = chip // 2, lax.rem(chip, 2)
    place = jnp.where(column == 0, up, 7 - up) - offset * (1 - 2 * core)
    place = lax.rem(place + 8, 8)
    return jnp.where(place < 4, 2 * place, 2 * (7 - place) + 1)


def foreign(offset):
    return chip_at(offset) // 4 != lax.axis_index("layer")


def put(out, at, offset, block):
    rows = block.shape[0] // 2
    core = lax.rem(lax.axis_index("row"), 2)
    if offset < 0:
        core = 1 - core
    start = (at - 4 * lax.axis_index("layer")) * 2 * rows
    out[pl.ds(pl.multiple_of(start + core * rows, rows), rows), :] = block[:rows]
    out[pl.ds(pl.multiple_of(start + (1 - core) * rows, rows), rows), :] = block[rows:]


def split(offset, ahead, behind, sent, kept):
    @pl.when(foreign(offset))
    def _():
        sent[...] = ahead[...].astype(sent.dtype)
        kept[...] = behind[...]

    @pl.when(jnp.logical_not(foreign(offset)))
    def _():
        sent[...] = behind[...].astype(sent.dtype)
        kept[...] = ahead[...]


def plain_kernel(turned, more, *refs):
    refs[-1][...] = score(turned, more, refs[:-1])


def second_kernel(turned, more, own, *refs):
    *queries, sent, kept, total = refs
    half = kept.shape[0]
    total[...] = score(turned, more, [*queries[:3], queries[3:]])
    split(2, total.at[:half], total.at[half:], sent.at[:half], kept)
    sent[half:] = own[...].astype(sent.dtype)


def third_kernel(turned, more, first, *refs):
    *queries, sent, kept, total = refs
    half = total.shape[0] // 2
    total[...] = score(turned, more, [*queries[:3], queries[3:]])
    split(1, first.at[:half], total.at[half:], sent.at[:half], kept.at[:half])
    split(3, total.at[:half], first.at[half:], sent.at[half:2 * half], kept.at[half:])


def opening_kernel(turned, *refs):
    unit, *swapped, out = refs

    @pl.when(foreign(4))
    def _():
        out[...] = layer_score(turned, [unit.at[0]] + [ref.at[0] for ref in swapped])


def second_layer(turned, opening, unit, swapped):
    return opening[...] + layer_score(turned, [unit.at[1]] + [ref.at[0] for ref in swapped])


def fourth_kernel(turned, opening, *refs):
    unit, *swapped, sent = refs

    @pl.when(foreign(4))
    def _():
        sent[...] = second_layer(turned, opening, unit, swapped).astype(sent.dtype)

    @pl.when(jnp.logical_not(foreign(4)))
    def _():
        sent[...] = jnp.zeros_like(sent)


def fifth_kernel(turned, more, *refs):
    unit, *swapped, kept = refs

    @pl.when(jnp.logical_not(foreign(4)))
    def _():
        kept[...] = score(turned, more, [unit, swapped])


def block_call(kernel, name, rows, total, turned, operands, kind=jnp.float32, sent=0):
    columns = turned[0].shape[1]
    block = jax.ShapeDtypeStruct((rows, columns), jnp.float32)
    one = total is None
    return pl.pallas_call(
        kernel,
        out_shape=(jax.ShapeDtypeStruct((max(rows, sent), columns), kind), block) if not one else jax.ShapeDtypeStruct(block.shape, kind),
        in_specs=[VMEM] * (len(turned) + len(operands)),
        out_specs=VMEM if one else (VMEM, VMEM),
        scratch_shapes=[pltpu.VMEM((total, columns), jnp.float32)] if total else [],
        compiler_params=pltpu.CompilerParams(vmem_limit_bytes=24 << 20),
        cost_estimate=pl.CostEstimate(flops=1 << 10, bytes_accessed=1 << 10, transcendentals=0),
        name=name,
    )(*turned, *operands)


def gather_kernel(kept2, got2, kept13, got13, own, out):
    rows = kept2.shape[0]
    low, high = pl.ds(0, rows), pl.ds(rows, rows)
    for offset, kept, got in (
        (2, kept2, got2.at[low]),
        (1, kept13.at[low], got13.at[low]),
        (3, kept13.at[high], got13.at[high]),
    ):
        block = kept[...] + got[...].astype(kept.dtype)

        @pl.when(foreign(offset))
        def _():
            put(out, chip_at(offset - 4), offset - 4, block)

        @pl.when(jnp.logical_not(foreign(offset)))
        def _():
            put(out, chip_at(offset), offset, block)

    @pl.when(foreign(4))
    def _():
        put(out, chip_at(0), 0, own[...] + got2[high].astype(own.dtype))


def last_kernel(kept, got, table, out, block, sem):
    del table

    @pl.when(jnp.logical_not(foreign(4)))
    def _():
        rows = kept.shape[0] // 2
        core = lax.rem(lax.axis_index("row"), 2)
        for n, c in enumerate((core, 1 - core)):
            part = pl.ds(n * rows, rows)
            block[pl.ds(pl.multiple_of(c * rows, rows), rows), :] = kept[part, :] + got[part, :].astype(kept.dtype)
        start = pl.multiple_of((chip_at(4) - 4 * lax.axis_index("layer")) * 2 * rows, 2 * rows)
        copy = pltpu.make_async_copy(block, out.at[pl.ds(start, 2 * rows)], sem)
        copy.start()
        copy.wait()


def finish(most, last, rows, columns):
    table = jax.ShapeDtypeStruct((rows, columns), jnp.float32)
    params = pltpu.CompilerParams(vmem_limit_bytes=8 << 20)
    gathered = pl.pallas_call(
        gather_kernel,
        out_shape=table,
        in_specs=[VMEM] * 5,
        out_specs=VMEM,
        compiler_params=params,
        cost_estimate=pl.CostEstimate(flops=60 << 30, bytes_accessed=1 << 20, transcendentals=0),
        name="gather_rows",
    )(*most)
    return pl.pallas_call(
        last_kernel,
        out_shape=table,
        in_specs=[VMEM, VMEM, HBM],
        out_specs=HBM,
        scratch_shapes=[pltpu.VMEM(last[0].shape, jnp.float32), pltpu.SemaphoreType.DMA],
        input_output_aliases={2: 0},
        compiler_params=params,
        name="last_rows",
    )(*last, gathered)


def ring_order(chips):
    wide = chips // 4
    order = [(i, 0) for i in range(4)]
    for turn, i in enumerate(reversed(range(4))):
        others = range(1, wide)
        order += [(i, j) for j in (reversed(others) if turn % 2 else others)]
    return [i * wide + j for i, j in order]


def ring_pairs(groups, chips, cores=2):
    order = ring_order(chips)
    flat = lambda layer, chip, core: (layer * chips + chip) * cores + core
    every = [(y, h, c) for y in range(groups) for h in range(chips) for c in range(cores)]
    step = lambda h, c: order[(order.index(h) + (1 - 2 * c)) % chips]
    swap = [(flat(y, h, c), flat(y, h, 1 - c)) for y, h, c in every]
    around = [(flat(y, h, c), flat(y, step(h, c), c)) for y, h, c in every]
    across = [(flat(y, h, c), flat(groups - 1 - y, h, c)) for y, h, c in every]
    return swap, around, across


def send(value, pairs):
    return lax.ppermute(value, AXES, pairs)


def any_ring_device(groups, chips, query_grads, train_grads, left_inverse, right_inverse):
    swap, around, _ = ring_pairs(groups, chips)
    order = ring_order(chips)
    mine = precondition(query_grads, left_inverse, right_inverse, True)
    turned = [transpose(l, train_grads) for l in range(query_grads.shape[0])]
    rows = mine.shape[1]
    row = lax.axis_index("row")
    chip, core = row // 2, lax.rem(row, 2)
    place = jnp.argmax(jnp.array(order, jnp.int32) == chip).astype(jnp.int32)
    table = jnp.zeros((chips * 2 * rows, train_grads.shape[1]), jnp.float32)

    def fill(table, block, offset, core):
        at = lax.rem(place + offset * (1 - 2 * lax.rem(row, 2)) + chips, chips)
        at = lax.dynamic_index_in_dim(jnp.array(order, jnp.int32), at, 0, keepdims=False) * 2 + core
        return lax.dynamic_update_slice_in_dim(table, block, at * rows, 0)

    held = [mine, send(mine, swap)]
    block = block_call(plain_kernel, "scores", 2 * rows, None, turned, held)
    table = fill(table, block[:rows], 0, core)
    table = fill(table, block[rows:], 0, 1 - core)
    for k in range(1, chips // 2 + 1):
        held = [send(h, around) for h in (held if k < chips // 2 else held[:1])]
        queries = held + [send(h, swap) for h in held]
        block = block_call(plain_kernel, "scores", len(queries) * rows, None, turned, queries)
        cores = (core, 1 - core, 1 - core, core) if len(held) == 2 else (core, 1 - core)
        for n, c in enumerate(cores):
            table = fill(table, block[n * rows:(n + 1) * rows], -k if n < len(held) or k == chips // 2 else k, c)
    return lax.psum_scatter(table, "layer", scatter_dimension=0, tiled=True)


def ring_device(query_grads, train_grads, left_inverse, right_inverse):
    chips, groups = 8, 2
    swap, around, across = ring_pairs(groups, chips)
    after = lax.optimization_barrier

    def quarters(unit):
        layers, held, feat = unit.shape
        half = held // 2
        return [send(unit[l:l + 1, n:n + half], swap) for l in range(layers) for n in (0, half)]

    halves_of = lambda unit: [send(unit[l:l + 1], swap) for l in range(unit.shape[0])]

    arrived = [send(query_grads, around), send(send(query_grads, swap), around)]
    mine = precondition(query_grads, left_inverse, right_inverse, True)
    a, b = [mine], [send(mine, swap)]
    turned = [transpose(l, train_grads) for l in range(2)]
    arrived[0], *turned = after((arrived[0], *turned))
    a.append(precondition(arrived[0], left_inverse, right_inverse, False))
    b.append(precondition(arrived[1], left_inverse, right_inverse, False))
    rows = 2 * mine.shape[1]
    zeroth = block_call(plain_kernel, "scores_0", rows, None, turned, [a[0], b[0]])
    a.append(send(a[1], around))
    b.append(send(b[1], around))
    first = block_call(plain_kernel, "scores_1", 2 * rows, None, turned, [a[1], b[1], send(a[1], swap), send(b[1], swap)])
    a.append(send(a[2], around))
    b[2], first, _ = after((b[2], first, mine))
    b.append(send(b[2], around))
    queries = [a[2], b[2], send(a[2], swap), *halves_of(b[2])]
    sent2, kept2 = block_call(second_kernel, "scores_2", rows, 2 * rows, turned, [zeroth] + queries, jnp.bfloat16, 2 * rows)
    a[3], _ = after((a[3], sent2))
    a.append(send(a[3], around))
    got2 = send(sent2, across)
    b[3], got2 = after((b[3], got2))
    queries = [a[3], b[3], send(a[3], swap), *halves_of(b[3])]
    sent, kept = block_call(third_kernel, "scores_3", 2 * rows, 2 * rows, turned, [first] + queries, jnp.bfloat16, 2 * rows + 32)
    got = send(sent, across)
    a[4], _ = after((a[4], sent))
    swapped = quarters(a[4])
    opening = block_call(opening_kernel, "scores_4", rows, None, turned[:1], [a[4], *swapped[:2]])
    sent4 = block_call(fourth_kernel, "scores_5", rows, None, turned[1:], [opening, a[4], *swapped[2:]], jnp.bfloat16)
    got4 = send(sent4, across)
    kept4 = block_call(fifth_kernel, "scores_6", rows, None, turned, [a[4], *swapped])
    return finish((kept2, got2, kept, got, zeroth), (kept4, got4), chips // groups * rows, turned[0].shape[1])


def solution(mesh):
    placed = (
        P("layer", "row", None),
        P("layer", "row", None),
        P("layer", None, None),
        P("layer", None, None),
    )
    groups, chips = mesh.shape["layer"], mesh.shape["row"] // 2
    if (groups, chips) == (2, 8):
        on_device = ring_device
    else:
        on_device = functools.partial(any_ring_device, groups, chips)
    return jax.shard_map(
        on_device, mesh=mesh, in_specs=placed, out_specs=P("layer", "row"), check_vma=False
    )
```

```python
import functools

import jax
import jax.numpy as jnp
from jax import lax
from jax.experimental import pallas as pl
from jax.experimental.pallas import tpu as pltpu
from jax.sharding import PartitionSpec as P

AXES = ("layer", "row")
VMEM = pl.BlockSpec(memory_space=pltpu.VMEM)
HBM = pl.BlockSpec(memory_space=pl.ANY)


def halves(v):
    top = v.astype(jnp.bfloat16)
    return top, (v - top.astype(jnp.float32)).astype(jnp.bfloat16)


def dot(a, b):
    return jnp.dot(a, b, preferred_element_type=jnp.float32)


def precondition_first_kernel(query_hbm, left_hbm, right_hbm, out, query, left, right, *refs):
    *scratch, sems = refs
    copies = [
        pltpu.make_async_copy(src, dst, sems.at[n])
        for n, (src, dst) in enumerate(((left_hbm, left), (right_hbm, right), (query_hbm, query)))
    ]
    for copy in copies:
        copy.start()
    copies[0].wait()
    copies[1].wait()
    precondition_kernel(query, left, right, out, *scratch, arrived=copies[2].wait)


def precondition_kernel(query, left, right, out, turned, mixed, arrived=lambda: None):
    layers, rows, feat = query.shape
    proj = left.shape[1]
    half, pairs, stride = proj // 2, feat // 128, mixed.shape[1] // (feat // 128)
    i = lax.broadcasted_iota(jnp.int32, (2 * proj, 4 * proj), 0) // proj
    j = lax.broadcasted_iota(jnp.int32, (2 * proj, 4 * proj), 1) // (2 * proj)
    same = i == j
    i = lax.broadcasted_iota(jnp.int32, (proj, proj), 0)
    j = lax.broadcasted_iota(jnp.int32, (proj, proj), 1)
    pick = (j == 2 * lax.rem(i, half) + i // half).astype(jnp.bfloat16)
    pick_t = (i == 2 * lax.rem(j, half) + j // half).astype(jnp.bfloat16)
    rights, lefts = [], []
    for l in range(layers):
        wide = jnp.concatenate([right[l], right[l]], axis=1)
        wide = jnp.concatenate([wide, wide], axis=1)
        wide = jnp.where(same, jnp.concatenate([wide, wide], axis=0), 0.0)
        rights.append(jnp.concatenate(halves(wide), axis=0))
        high, low = halves(left[l])
        both = dot(pick, jnp.concatenate([high, low], axis=1)).astype(jnp.bfloat16)
        high, low = (dot(both[:, n:n + proj], pick_t).astype(jnp.bfloat16) for n in (0, proj))
        lefts.append(jnp.concatenate([high, low, high], axis=1))
    arrived()
    for l in range(layers):
        x = jnp.concatenate([query[l, :, k * 128:(k + 1) * 128] for k in range(pairs)], axis=0)
        y = dot(jnp.concatenate([x, x], axis=1), rights[l])
        for p in range(2):
            for k in range(pairs):
                turned[l, p, k * stride:k * stride + rows] = y[k * rows:(k + 1) * rows, p * 128:(p + 1) * 128]
    step = 8
    first = lax.rem(lax.broadcasted_iota(jnp.int32, (pairs, step * 128), 1), 128) < proj
    for l in range(layers):
        for q in range(0, rows, step):
            y = [
                jnp.concatenate([turned[l, p, pl.ds(q + n, pairs, stride=stride), :] for n in range(step)], axis=1)
                for p in range(2)
            ]
            high, low = halves(jnp.concatenate(y, axis=0))
            z = dot(lefts[l], jnp.concatenate([high, high, low], axis=0))
            z = jnp.where(first, z[:half], z[half:])
            for n in range(step):
                mixed[l, pl.ds(q + n, pairs, stride=stride), :] = z[:, n * 128:(n + 1) * 128]
        for m in range(pairs):
            out[l, :, m * 128:(m + 1) * 128] = mixed[l, m * stride:m * stride + rows].astype(jnp.bfloat16)


def precondition(query, left, right, first):
    layers, rows, feat = query.shape
    spread = (rows + 8) * feat // 128
    scratch = [pltpu.VMEM((layers, 2, spread, 128), jnp.float32), pltpu.VMEM((layers, spread, 128), jnp.float32)]
    operands = (query, left, right)
    if first:
        scratch = [pltpu.VMEM(v.shape, v.dtype) for v in operands] + scratch + [pltpu.SemaphoreType.DMA((3,))]
        operands = [pltpu.with_memory_space_constraint(v, pltpu.HBM) for v in operands]
    return pl.pallas_call(
        precondition_first_kernel if first else precondition_kernel,
        out_shape=jax.ShapeDtypeStruct(query.shape, jnp.bfloat16),
        in_specs=[HBM if first else VMEM] * 3,
        out_specs=VMEM,
        scratch_shapes=scratch,
        compiler_params=pltpu.CompilerParams(vmem_limit_bytes=16 << 20),
        cost_estimate=pl.CostEstimate(flops=2 << 30, bytes_accessed=4 << 20, transcendentals=0),
        name="precondition_0" if first else "precondition_1",
    )(*operands)


def transpose_kernel(layer, train, out, buffer, sems):
    feat = train.shape[2]
    deep, rows, wide = buffer.shape
    steps = feat // wide

    def copy(n):
        return pltpu.make_async_copy(train.at[layer, :, pl.ds(n * wide, wide)], buffer.at[n % deep], sems.at[n % deep])

    for n in range(deep):
        copy(n).start()
    for n in range(steps):
        copy(n).wait()
        out[n * wide:(n + 1) * wide, :] = buffer[n % deep].T
        if n + deep < steps:
            copy(n + deep).start()


def transpose(layer, train):
    layers, rows, feat = train.shape
    wide, deep = 512, 8
    return pl.pallas_call(
        functools.partial(transpose_kernel, layer),
        out_shape=pltpu.VMEM((feat, rows), train.dtype),
        in_specs=[HBM],
        out_specs=VMEM,
        scratch_shapes=[pltpu.VMEM((deep, rows, wide), train.dtype), pltpu.SemaphoreType.DMA((deep,))],
        compiler_params=pltpu.CompilerParams(vmem_limit_bytes=16 << 20),
        cost_estimate=pl.CostEstimate(flops=2 << 30, bytes_accessed=8 << 20, transcendentals=0),
        name="transpose_%d" % layer,
    )(pltpu.with_memory_space_constraint(train, pltpu.HBM))


def layer_score(turned, rows):
    rows = [row[...] for row in rows]
    count = sum(row.shape[0] for row in rows)
    rows = rows * max(1, 128 // count)
    return dot(jnp.concatenate(rows, axis=0), turned[...])[:count]


def pieces(unit, layer):
    if not isinstance(unit, (list, tuple)):
        return [unit.at[layer]]
    half = len(unit) // 2
    return [piece.at[0] for piece in unit[layer * half:(layer + 1) * half]]


def score(turned, more, units):
    return sum(
        layer_score(t, [piece for unit in units for piece in pieces(unit, layer)])
        for layer, t in enumerate((turned, more))
    )


def chip_at(offset):
    row = lax.axis_index("row")
    chip, core = row // 2, lax.rem(row, 2)
    up, column = chip // 2, lax.rem(chip, 2)
    place = jnp.where(column == 0, up, 7 - up) - offset * (1 - 2 * core)
    place = lax.rem(place + 8, 8)
    return jnp.where(place < 4, 2 * place, 2 * (7 - place) + 1)


def foreign(offset):
    return chip_at(offset) // 4 != lax.axis_index("layer")


def put(out, at, offset, block):
    rows = block.shape[0] // 2
    core = lax.rem(lax.axis_index("row"), 2)
    if offset < 0:
        core = 1 - core
    start = (at - 4 * lax.axis_index("layer")) * 2 * rows
    out[pl.ds(pl.multiple_of(start + core * rows, rows), rows), :] = block[:rows]
    out[pl.ds(pl.multiple_of(start + (1 - core) * rows, rows), rows), :] = block[rows:]


def split(offset, ahead, behind, sent, kept):
    @pl.when(foreign(offset))
    def _():
        sent[...] = ahead[...].astype(sent.dtype)
        kept[...] = behind[...]

    @pl.when(jnp.logical_not(foreign(offset)))
    def _():
        sent[...] = behind[...].astype(sent.dtype)
        kept[...] = ahead[...]


def plain_kernel(turned, more, *refs):
    refs[-1][...] = score(turned, more, refs[:-1])


def second_kernel(turned, more, own, *refs):
    *queries, sent, kept, total = refs
    half = kept.shape[0]
    total[...] = score(turned, more, [*queries[:3], queries[3:]])
    split(2, total.at[:half], total.at[half:], sent.at[:half], kept)
    sent[half:] = own[...].astype(sent.dtype)


def third_kernel(turned, more, first, *refs):
    *queries, sent, kept, total = refs
    half = total.shape[0] // 2
    total[...] = score(turned, more, [*queries[:3], queries[3:]])
    split(1, first.at[:half], total.at[half:], sent.at[:half], kept.at[:half])
    split(3, total.at[:half], first.at[half:], sent.at[half:2 * half], kept.at[half:])


def opening_kernel(turned, *refs):
    unit, *swapped, out = refs
    out[...] = layer_score(turned, [unit.at[0]] + [ref.at[0] for ref in swapped])


def second_layer(turned, opening, unit, swapped):
    return opening[...] + layer_score(turned, [unit.at[1]] + [ref.at[0] for ref in swapped])


def fourth_kernel(turned, opening, *refs):
    unit, *swapped, sent = refs

    @pl.when(foreign(4))
    def _():
        sent[...] = second_layer(turned, opening, unit, swapped).astype(sent.dtype)

    @pl.when(jnp.logical_not(foreign(4)))
    def _():
        sent[...] = jnp.zeros_like(sent)


def fifth_kernel(turned, opening, *refs):
    unit, *swapped, kept = refs

    @pl.when(jnp.logical_not(foreign(4)))
    def _():
        kept[...] = second_layer(turned, opening, unit, swapped)


def block_call(kernel, name, rows, total, turned, operands, kind=jnp.float32, sent=0):
    columns = turned[0].shape[1]
    block = jax.ShapeDtypeStruct((rows, columns), jnp.float32)
    one = total is None
    return pl.pallas_call(
        kernel,
        out_shape=(jax.ShapeDtypeStruct((max(rows, sent), columns), kind), block) if not one else jax.ShapeDtypeStruct(block.shape, kind),
        in_specs=[VMEM] * (len(turned) + len(operands)),
        out_specs=VMEM if one else (VMEM, VMEM),
        scratch_shapes=[pltpu.VMEM((total, columns), jnp.float32)] if total else [],
        compiler_params=pltpu.CompilerParams(vmem_limit_bytes=24 << 20),
        cost_estimate=pl.CostEstimate(flops=1 << 10, bytes_accessed=1 << 10, transcendentals=0),
        name=name,
    )(*turned, *operands)


def gather_kernel(kept2, got2, kept13, got13, own, out):
    rows = kept2.shape[0]
    low, high = pl.ds(0, rows), pl.ds(rows, rows)
    for offset, kept, got in (
        (2, kept2, got2.at[low]),
        (1, kept13.at[low], got13.at[low]),
        (3, kept13.at[high], got13.at[high]),
    ):
        block = kept[...] + got[...].astype(kept.dtype)

        @pl.when(foreign(offset))
        def _():
            put(out, chip_at(offset - 4), offset - 4, block)

        @pl.when(jnp.logical_not(foreign(offset)))
        def _():
            put(out, chip_at(offset), offset, block)

    @pl.when(foreign(4))
    def _():
        put(out, chip_at(0), 0, own[...] + got2[high].astype(own.dtype))


def last_kernel(kept, got, table, out, block, sem):
    del table

    @pl.when(jnp.logical_not(foreign(4)))
    def _():
        rows = kept.shape[0] // 2
        core = lax.rem(lax.axis_index("row"), 2)
        for n, c in enumerate((core, 1 - core)):
            part = pl.ds(n * rows, rows)
            block[pl.ds(pl.multiple_of(c * rows, rows), rows), :] = kept[part, :] + got[part, :].astype(kept.dtype)
        start = pl.multiple_of((chip_at(4) - 4 * lax.axis_index("layer")) * 2 * rows, 2 * rows)
        copy = pltpu.make_async_copy(block, out.at[pl.ds(start, 2 * rows)], sem)
        copy.start()
        copy.wait()


def finish(most, last, rows, columns):
    table = jax.ShapeDtypeStruct((rows, columns), jnp.float32)
    params = pltpu.CompilerParams(vmem_limit_bytes=8 << 20)
    gathered = pl.pallas_call(
        gather_kernel,
        out_shape=table,
        in_specs=[VMEM] * 5,
        out_specs=VMEM,
        compiler_params=params,
        cost_estimate=pl.CostEstimate(flops=60 << 30, bytes_accessed=1 << 20, transcendentals=0),
        name="gather_rows",
    )(*most)
    return pl.pallas_call(
        last_kernel,
        out_shape=table,
        in_specs=[VMEM, VMEM, HBM],
        out_specs=HBM,
        scratch_shapes=[pltpu.VMEM(last[0].shape, jnp.float32), pltpu.SemaphoreType.DMA],
        input_output_aliases={2: 0},
        compiler_params=params,
        name="last_rows",
    )(*last, gathered)


def ring_order(chips):
    wide = chips // 4
    order = [(i, 0) for i in range(4)]
    for turn, i in enumerate(reversed(range(4))):
        others = range(1, wide)
        order += [(i, j) for j in (reversed(others) if turn % 2 else others)]
    return [i * wide + j for i, j in order]


def ring_pairs(groups, chips, cores=2):
    order = ring_order(chips)
    flat = lambda layer, chip, core: (layer * chips + chip) * cores + core
    every = [(y, h, c) for y in range(groups) for h in range(chips) for c in range(cores)]
    step = lambda h, c: order[(order.index(h) + (1 - 2 * c)) % chips]
    swap = [(flat(y, h, c), flat(y, h, 1 - c)) for y, h, c in every]
    around = [(flat(y, h, c), flat(y, step(h, c), c)) for y, h, c in every]
    across = [(flat(y, h, c), flat(groups - 1 - y, h, c)) for y, h, c in every]
    return swap, around, across


def send(value, pairs):
    return lax.ppermute(value, AXES, pairs)


def any_ring_device(groups, chips, query_grads, train_grads, left_inverse, right_inverse):
    swap, around, _ = ring_pairs(groups, chips)
    order = ring_order(chips)
    mine = precondition(query_grads, left_inverse, right_inverse, True)
    turned = [transpose(l, train_grads) for l in range(query_grads.shape[0])]
    rows = mine.shape[1]
    row = lax.axis_index("row")
    chip, core = row // 2, lax.rem(row, 2)
    place = jnp.argmax(jnp.array(order, jnp.int32) == chip).astype(jnp.int32)
    table = jnp.zeros((chips * 2 * rows, train_grads.shape[1]), jnp.float32)

    def fill(table, block, offset, core):
        at = lax.rem(place + offset * (1 - 2 * lax.rem(row, 2)) + chips, chips)
        at = lax.dynamic_index_in_dim(jnp.array(order, jnp.int32), at, 0, keepdims=False) * 2 + core
        return lax.dynamic_update_slice_in_dim(table, block, at * rows, 0)

    held = [mine, send(mine, swap)]
    block = block_call(plain_kernel, "scores", 2 * rows, None, turned, held)
    table = fill(table, block[:rows], 0, core)
    table = fill(table, block[rows:], 0, 1 - core)
    for k in range(1, chips // 2 + 1):
        held = [send(h, around) for h in (held if k < chips // 2 else held[:1])]
        queries = held + [send(h, swap) for h in held]
        block = block_call(plain_kernel, "scores", len(queries) * rows, None, turned, queries)
        cores = (core, 1 - core, 1 - core, core) if len(held) == 2 else (core, 1 - core)
        for n, c in enumerate(cores):
            table = fill(table, block[n * rows:(n + 1) * rows], -k if n < len(held) or k == chips // 2 else k, c)
    return lax.psum_scatter(table, "layer", scatter_dimension=0, tiled=True)


def ring_device(query_grads, train_grads, left_inverse, right_inverse):
    chips, groups = 8, 2
    swap, around, across = ring_pairs(groups, chips)
    after = lax.optimization_barrier

    def quarters(unit):
        layers, held, feat = unit.shape
        half = held // 2
        return [send(unit[l:l + 1, n:n + half], swap) for l in range(layers) for n in (0, half)]

    halves_of = lambda unit: [send(unit[l:l + 1], swap) for l in range(unit.shape[0])]

    arrived = [send(query_grads, around), send(send(query_grads, swap), around)]
    mine = precondition(query_grads, left_inverse, right_inverse, True)
    a, b = [mine], [send(mine, swap)]
    turned = [transpose(l, train_grads) for l in range(2)]
    arrived[0], *turned = after((arrived[0], *turned))
    a.append(precondition(arrived[0], left_inverse, right_inverse, False))
    b.append(precondition(arrived[1], left_inverse, right_inverse, False))
    rows = 2 * mine.shape[1]
    zeroth = block_call(plain_kernel, "scores_0", rows, None, turned, [a[0], b[0]])
    a.append(send(a[1], around))
    b.append(send(b[1], around))
    first = block_call(plain_kernel, "scores_1", 2 * rows, None, turned, [a[1], b[1], send(a[1], swap), send(b[1], swap)])
    a.append(send(a[2], around))
    b[2], first, _ = after((b[2], first, mine))
    b.append(send(b[2], around))
    queries = [a[2], b[2], send(a[2], swap), *halves_of(b[2])]
    sent2, kept2 = block_call(second_kernel, "scores_2", rows, 2 * rows, turned, [zeroth] + queries, jnp.bfloat16, 2 * rows)
    a[3], _ = after((a[3], sent2))
    a.append(send(a[3], around))
    got2 = send(sent2, across)
    b[3], got2 = after((b[3], got2))
    queries = [a[3], b[3], send(a[3], swap), *halves_of(b[3])]
    sent, kept = block_call(third_kernel, "scores_3", 2 * rows, 2 * rows, turned, [first] + queries, jnp.bfloat16, 2 * rows + 32)
    got = send(sent, across)
    a[4], _ = after((a[4], sent))
    swapped = quarters(a[4])
    opening = block_call(opening_kernel, "scores_4", rows, None, turned[:1], [a[4], *swapped[:2]])
    sent4 = block_call(fourth_kernel, "scores_5", rows, None, turned[1:], [opening, a[4], *swapped[2:]], jnp.bfloat16)
    got4 = send(sent4, across)
    kept4 = block_call(fifth_kernel, "scores_6", rows, None, turned[1:], [opening, a[4], *swapped[2:]])
    return finish((kept2, got2, kept, got, zeroth), (kept4, got4), chips // groups * rows, turned[0].shape[1])


def solution(mesh):
    placed = (
        P("layer", "row", None),
        P("layer", "row", None),
        P("layer", None, None),
        P("layer", None, None),
    )
    groups, chips = mesh.shape["layer"], mesh.shape["row"] // 2
    if (groups, chips) == (2, 8):
        on_device = ring_device
    else:
        on_device = functools.partial(any_ring_device, groups, chips)
    return jax.shard_map(
        on_device, mesh=mesh, in_specs=placed, out_specs=P("layer", "row"), check_vma=False
    )
```
